256 devices in a mesh: dp: 32 (over x, z_hi, core), fisher: 8 (over z_lo, y).
Axes of the slice: x: 4, y: 4, z: 8 (z_hi: 4, z_lo: 2; z = z_hi * 2 + z_lo), core: 2. Of those that a mesh axis runs over, the one named last changes fastest.
Arguments:
- acts: bfloat16 [65536, 4096], P('dp', 'fisher'), may hold values from -6 to 6
- cotangent: bfloat16 [65536, 4096], P('dp'), may hold values from -6 to 6
- out_weight: bfloat16 [4096, 4096], P('fisher', 'dp'), may hold values from -0.09375 to 0.09375
- proj_in: bfloat16 [4096, 64], P('fisher'), may hold values from -0.09375 to 0.09375
- proj_out: bfloat16 [4096, 64], replicated, may hold values from -0.09375 to 0.09375
- panels: bfloat16 [4096, 4096], P('dp', 'fisher'), may hold values from -0.09375 to 0.09375
Outputs:
- act_grad: bfloat16 [65536, 4096], P('dp', 'fisher')
- fisher_tile: float32 [4096, 4096], P('dp', 'fisher')
- scores: float32 [128, 4096], P('dp', 'fisher')
The draws below stay inside these ranges and needn't reach their ends.
All inputs are finite; a program needn't handle non-finite values.
Results may differ from the reference program's by a relative error of at most 0.0048.
Values may be sent and summed in bfloat16 or wider, within the bound.
A program may use at most 128 MiB of HBM per device.

```python
import math
import jax
import jax.numpy as jnp
from jax import lax

D = 4096
K_OUT = 64
K_IN = 64
LEN = 512
K = 4096
EXAMPLES = 128
TOKENS = 65536
QUERIES = 4096


def block_levels(own_key, dims, shards, least, high):
    level = 1.0
    for position, parts in shards:
        steps = jax.random.uniform(jax.random.fold_in(jax.random.fold_in(own_key, 6), position), (parts,), jnp.float32, least / len(shards), high / len(shards))
        level = level * jnp.repeat(jnp.exp(steps), dims[position] // parts).reshape((-1,) + (1,) * (len(dims) - 1 - position))
    return level


def bell_draw(key, shape, scale, bound, pieces=(), kind=jnp.bfloat16):
    loudness = block_levels(key, shape, pieces, -0.22, 0.18) if pieces else 1.0
    array = jax.random.normal(key, shape, jnp.float32) * scale * loudness
    return jnp.minimum(jnp.maximum(array, -bound), bound).astype(kind)


def setup_inputs(seed: int = 0) -> dict:
    arg_keys = jax.random.split(jax.random.key(seed), 7)
    return {
        "acts": bell_draw(arg_keys[0], (TOKENS, D), 1.0, 6.0, ((0, 32), (1, 8))),
        "cotangent": bell_draw(arg_keys[1], (TOKENS, D), 1.0, 6.0, ((0, 32),)),
        "out_weight": bell_draw(arg_keys[2], (D, D), D ** -0.5, 0.09375, ((0, 8), (1, 32))),
        "proj_in": bell_draw(arg_keys[3], (D, K_IN), D ** -0.5, 0.09375, ((0, 8),)),
        "proj_out": bell_draw(arg_keys[4], (D, K_OUT), D ** -0.5, 0.09375),
        "panels": bell_draw(arg_keys[5], (K, QUERIES), K ** -0.5, 0.09375, ((0, 32), (1, 8))),
    }


def reference(acts, cotangent, out_weight, proj_in, proj_out, panels):
    act_grad = lax.dot_general(cotangent, out_weight, (((1,), (1,)), ((), ())), preferred_element_type=jnp.float32).astype(jnp.bfloat16)
    in_proj = jnp.dot(acts, proj_in, preferred_element_type=jnp.float32)
    out_proj = jnp.dot(cotangent, proj_out, preferred_element_type=jnp.float32)
    in_each = in_proj.reshape(EXAMPLES, LEN, K_IN)
    out_each = out_proj.reshape(EXAMPLES, LEN, K_OUT)
    summed = jnp.einsum('eta,etb->eab', out_each, in_each, precision=lax.Precision.HIGHEST)
    grads = (summed * (1.0 / math.sqrt(LEN))).reshape(EXAMPLES, K_OUT * K_IN).astype(jnp.bfloat16)
    gram = lax.dot_general(grads, grads, (((0,), (0,)), ((), ())), preferred_element_type=jnp.float32)
    fisher_tile = gram * (1.0 / EXAMPLES)
    scores = jnp.dot(grads, panels, preferred_element_type=jnp.float32)
    return (act_grad, fisher_tile, scores)
```

```python
import math

import jax
import jax.numpy as jnp
from jax import lax
from jax.sharding import PartitionSpec as P

LEN = 512


def contract_rows(left, right):
    return lax.dot_general(
        left, right, (((0,), (0,)), ((), ())), preferred_element_type=jnp.float32
    )


def per_device(acts, cotangent, out_weight, proj_in, proj_out, panels):
    tok_rows = acts.shape[0]
    width_in = proj_in.shape[1]
    width_out = proj_out.shape[1]
    width_all = width_in * width_out
    ex_local = tok_rows // LEN
    dp_count = lax.axis_size("dp")
    fisher_count = lax.axis_size("fisher")
    dp_place = lax.axis_index("dp")
    fisher_place = lax.axis_index("fisher")
    examples_all = ex_local * dp_count
    in_part = jnp.dot(acts, proj_in, preferred_element_type=jnp.float32)
    out_proj = jnp.dot(cotangent, proj_out, preferred_element_type=jnp.float32)
    out_each = out_proj.reshape(ex_local, LEN, width_out)
    in_each = in_part.reshape(ex_local, LEN, width_in)
    part = jnp.einsum("eta,etb->eab", out_each, in_each, precision=lax.Precision.HIGHEST)
    summed = lax.psum(part, "fisher")
    grads = (summed * (1.0 / math.sqrt(LEN))).reshape(ex_local, width_all).astype(jnp.bfloat16)
    everyone = lax.all_gather(grads, "dp", axis=0, tiled=True)
    tile_cols = width_all // fisher_count
    tile_rows = width_all // dp_count
    col_block = lax.dynamic_slice_in_dim(everyone, fisher_place * tile_cols, tile_cols, 1)
    row_block = lax.dynamic_slice_in_dim(everyone, dp_place * tile_rows, tile_rows, 1)
    fisher_tile = contract_rows(row_block, col_block) * (1.0 / examples_all)
    score_part = jnp.dot(row_block, panels, preferred_element_type=jnp.float32)
    scores = lax.psum_scatter(score_part, "dp", scatter_dimension=0, tiled=True)
    act_grad = lax.dot_general(
        cotangent,
        lax.all_gather(out_weight, "dp", axis=1, tiled=True),
        (((1,), (1,)), ((), ())),
        preferred_element_type=jnp.float32,
    ).astype(jnp.bfloat16)
    return (act_grad, fisher_tile, scores)


def solution(mesh):
    return jax.shard_map(
        per_device,
        mesh=mesh,
        in_specs=(
            P("dp", "fisher"),
            P("dp", None),
            P("fisher", "dp"),
            P("fisher", None),
            P(),
            P("dp", "fisher"),
        ),
        out_specs=(P("dp", "fisher"), P("dp", "fisher"), P("dp", "fisher")),
        check_vma=False,
    )
```

```python
import functools
import math

import jax
import jax.numpy as jnp
from jax import lax
from jax.experimental import pallas as pl
from jax.experimental.pallas import tpu as pltpu
from jax.sharding import PartitionSpec as P

LEN = 512
MESH = pl.DeviceIdType.MESH
F32 = jnp.float32
BF16 = jnp.bfloat16
ROWS = 512


def dot(a, b, ca=1, cb=0, precision=None):
    return lax.dot_general(
        a, b, (((ca,), (cb,)), ((), ())), preferred_element_type=F32, precision=precision
    )


def kernel(
    acts_h, cot_h, w_h, pin_h, pout_h, pan_h,
    act_o, fish_o, score_o,
    acts, cot, w_own, pin, pout, pan,
    wg, acc, act_v,
    q_part, send1, recv1, g_own, g_row, send2, g_all, s_part, s_pair, s_sum, recv3, fin,
    in_sem, cot_sem, out_sem,
    w_send, rz, rx, rsib,
    e_send, e_recv,
):
    i = lax.axis_index("dp")
    j = lax.axis_index("fisher")
    c = lax.rem(i, 2)
    q = i // 2
    zh = lax.rem(q, 4)
    x = q // 4
    sib = (i + 1 - 2 * c, j)

    def chip(dx, dz):
        return lax.rem(x + dx + 4, 4) * 4 + lax.rem(zh + dz + 4, 4)

    def dev(dx, dz):
        return (chip(dx, dz) * 2 + c, j)

    loads = [
        pltpu.make_async_copy(w_h, w_own, in_sem.at[0]),
        pltpu.make_async_copy(pout_h, pout, in_sem.at[1]),
        pltpu.make_async_copy(pin_h, pin, in_sem.at[2]),
        pltpu.make_async_copy(acts_h, acts, in_sem.at[3]),
        pltpu.make_async_copy(pan_h, pan, in_sem.at[4]),
    ]
    for load in loads[:4]:
        load.start()

    def cot_load(e):
        rows = pl.ds(e * LEN, LEN)
        return pltpu.make_async_copy(cot_h.at[rows], cot.at[rows], cot_sem.at[e])

    for e in range(4):
        cot_load(e).start()
    loads[4].start()

    barrier = pltpu.get_barrier_semaphore()
    pl.semaphore_signal(barrier, inc=1, device_id=sib, device_id_type=MESH)

    @pl.loop(1, 8)
    def _(s):
        pl.semaphore_signal(barrier, inc=1, device_id=(i, lax.rem(j + s, 8)), device_id_type=MESH)

    @pl.loop(1, 16)
    def _(s):
        pl.semaphore_signal(
            barrier, inc=1, device_id=(lax.rem(q + s, 16) * 2 + c, j), device_id_type=MESH
        )

    eye = jnp.where(
        lax.broadcasted_iota(jnp.int32, (128, 128), 0) == lax.broadcasted_iota(jnp.int32, (128, 128), 1),
        1.0, 0.0,
    ).astype(BF16)
    loads[0].wait()

    def wrows(chip_index, core, half=None):
        start = chip_index * 256 + core * 128
        if half is None:
            return wg.at[pl.ds(pl.multiple_of(start, 128), 128)]
        return wg.at[pl.ds(pl.multiple_of(start + 64 * half, 64), 64)]

    wg[pl.ds(pl.multiple_of(q * 256 + c * 128, 128), 128), :] = dot(eye, w_own[...], 1, 1).astype(BF16)
    pl.semaphore_wait(barrier, 23)

    sent = []

    def push(ref, to, recv):
        copy = pltpu.make_async_remote_copy(
            src_ref=ref, dst_ref=ref, send_sem=w_send.at[len(sent)], recv_sem=recv,
            device_id=to, device_id_type=MESH,
        )
        copy.start()
        sent.append(copy)

    def arrive(ref, sem):
        pltpu.make_async_copy(ref, ref, sem).wait()

    DZ = (0, -1, 1, 2)
    DX = (0, -1, 1, 2)

    def to_x(m):
        push(wrows(chip(0, DZ[m]), c), dev(1, 0), rx.at[m, 0])
        push(wrows(chip(0, DZ[m]), c), dev(-1, 0), rx.at[m, 1])

    def to_sib(m, k):
        push(wrows(chip(DX[k], DZ[m]), c), sib, rsib.at[m, k])

    push(wrows(q, c), dev(0, 1), rz.at[0])
    push(wrows(q, c), dev(0, -1), rz.at[1])
    to_x(0)
    to_sib(0, 0)

    def x_near(m):
        arrive(wrows(chip(-1, DZ[m]), c), rx.at[m, 0])
        push(wrows(chip(-1, DZ[m]), c, 0), dev(1, 0), rx.at[m, 2])
        to_sib(m, 1)
        arrive(wrows(chip(1, DZ[m]), c), rx.at[m, 1])
        push(wrows(chip(1, DZ[m]), c, 1), dev(-1, 0), rx.at[m, 3])
        to_sib(m, 2)

    def x_far(m):
        arrive(wrows(chip(2, DZ[m]), c, 0), rx.at[m, 2])
        arrive(wrows(chip(2, DZ[m]), c, 1), rx.at[m, 3])
        to_sib(m, 3)

    def z_near():
        arrive(wrows(chip(0, -1), c), rz.at[0])
        push(wrows(chip(0, -1), c, 0), dev(0, 1), rz.at[2])
        to_x(1)
        arrive(wrows(chip(0, 1), c), rz.at[1])
        push(wrows(chip(0, 1), c, 1), dev(0, -1), rz.at[3])
        to_x(2)
        to_sib(1, 0)
        to_sib(2, 0)

    def z_far():
        arrive(wrows(chip(0, 2), c, 0), rz.at[2])
        arrive(wrows(chip(0, 2), c, 1), rz.at[3])
        to_x(3)
        to_sib(3, 0)

    loads[1].wait()
    row = lax.broadcasted_iota(jnp.int32, (64, 64), 0)
    col = lax.broadcasted_iota(jnp.int32, (64, 64), 1)
    even_odd = jnp.where(col == lax.rem(row, 32) * 2 + row // 32, 1.0, 0.0).astype(BF16)
    pout[...] = dot(even_odd, pout[...]).astype(BF16)
    loads[2].wait()
    loads[3].wait()

    def example(e, _):
        cot_load(e).wait()
        rows = pl.ds(pl.multiple_of(e * LEN, LEN), LEN)
        op = dot(cot[rows, :], pout[...], 1, 1)
        ip = dot(acts[rows, :], pin[...], 1, 1)
        part = dot(op, ip, 0, 0, lax.Precision.HIGHEST)
        q_part[e] = jnp.concatenate([part[:32], part[32:]], axis=1)
        return 0

    lax.fori_loop(0, 2, example, 0)
    x_near(0)
    lax.fori_loop(2, 4, example, 0)
    z_near()
    for jj in range(8):
        for e in range(4):
            send1[jj, e * 4:e * 4 + 4, :] = q_part[e, jj * 4:jj * 4 + 4, :]

    def exchange(n, copy_of, stage):
        def go(s, _):
            copy_of(s).start()
            return 0
        lax.fori_loop(1, n, go, 0)

    def done_sending(n, copy_of):
        def go(s, _):
            copy_of(s).wait_send()
            return 0
        lax.fori_loop(1, n, go, 0)

    def remote(src, dst, to, stage, s):
        return pltpu.make_async_remote_copy(
            src_ref=src, dst_ref=dst, send_sem=e_send.at[stage, s], recv_sem=e_recv.at[stage],
            device_id=to, device_id_type=MESH,
        )

    def copy1(s):
        to = lax.rem(j + s, 8)
        return remote(send1.at[to], recv1.at[j], (i, to), 0, s)

    def copy1b(s):
        return remote(g_own, g_row.at[j], (i, lax.rem(j + s, 8)), 1, s)

    def copy2(s):
        to = lax.rem(q + s, 16)
        return remote(send2.at[to], g_all.at[c, q], (to * 2 + c, j), 2, s)

    def copy2c():
        return remote(g_all.at[c], g_all.at[c], sib, 3, 0)

    def copy3c():
        return remote(s_part.at[1 - c], s_pair, sib, 4, 0)

    def copy3(s):
        to = lax.rem(q + s, 16)
        rows = pl.ds(pl.multiple_of(to * 8, 8), 8)
        return remote(s_sum.at[rows], recv3.at[q], (to * 2 + c, j), 5, s)

    def copy3f():
        return remote(fin.at[c], fin.at[c], sib, 6, 0)

    def blocks(m, k):
        if (m, k) != (0, 0):
            pass
        arrive(wrows(chip(DX[k], DZ[m]), 1 - c), rsib.at[m, k])

    def a_pass(first, second, mode):
        blocks(*first)
        blocks(*second)
        ka = pl.ds(pl.multiple_of(chip(DX[first[1]], DZ[first[0]]) * 256, 256), 256)
        kb = pl.ds(pl.multiple_of(chip(DX[second[1]], DZ[second[0]]) * 256, 256), 256)

        def step(t, _):
            rows = pl.ds(pl.multiple_of(t * ROWS, ROWS), ROWS)
            new = dot(cot[rows, ka], wg[ka, :]) + dot(cot[rows, kb], wg[kb, :])
            if mode == 0:
                acc[rows, :] = new
            elif mode == 1:
                acc[rows, :] += new
            else:
                act_v[rows, :] = (acc[rows, :] + new).astype(BF16)
                pltpu.make_async_copy(act_v.at[rows], act_o.at[rows], out_sem.at[t]).start()
            return 0

        lax.fori_loop(0, acc.shape[0] // ROWS, step, 0)

    exchange(8, copy1, 0)
    recv1[j] = send1[j]
    x_far(0)
    a_pass((0, 0), (0, 1), 0)

    arrive(recv1.at[pl.ds(0, 7)], e_recv.at[0])
    total = recv1[0]
    for s in range(1, 8):
        total = total + recv1[s]
    mine = (total * (1.0 / math.sqrt(LEN))).astype(BF16)
    g_own[...] = mine
    exchange(8, copy1b, 1)
    g_row[j] = mine
    z_far()
    a_pass((0, 2), (1, 0), 1)
    x_near(1)

    arrive(g_row.at[pl.ds(0, 7)], e_recv.at[1])
    for to in range(16):
        send2[to, 0] = g_row[to // 2]
        send2[to, 1] = mine
    exchange(16, copy2, 2)
    g_all[c, q] = send2[q]
    x_near(2)
    a_pass((2, 0), (0, 3), 1)

    arrive(g_all.at[c, pl.ds(0, 15)], e_recv.at[2])
    copy2c().start()
    x_far(1)
    a_pass((3, 0), (1, 1), 1)
    x_far(2)

    arrive(g_all.at[1 - c], e_recv.at[3])
    m = lax.broadcasted_iota(jnp.int32, (128, 512), 0)
    n = lax.broadcasted_iota(jnp.int32, (128, 512), 1)
    base = lax.rem(m // 4, 2) * 256 + (m // 8) * 16 + lax.rem(m, 4) * 4

    def select(r):
        return jnp.where(n == base + r, 1.0, 0.0).astype(BF16)

    row_tiles = g_all[:, :, 0].reshape(512, 128)
    col_tiles = g_all[:, :, 1].reshape(512, 128)
    g_rows = dot(select(lax.rem(i, 4)), row_tiles).astype(BF16)
    loads[4].wait()
    s_part[0] = dot(g_rows, pan[:, :256])
    s_part[1] = dot(g_rows, pan[:, 256:])
    copy3c().start()
    for r in range(4):
        g_cols = dot(select(r), col_tiles).astype(BF16)
        fish_o[:, r * 128:(r + 1) * 128] = dot(g_rows, g_cols, 0, 0) * (1.0 / 128)
    x_near(3)
    a_pass((1, 2), (2, 1), 1)

    arrive(s_pair, e_recv.at[4])
    s_sum[...] = s_part[c] + s_pair[...]
    exchange(16, copy3, 5)
    recv3[q] = s_sum[pl.ds(pl.multiple_of(q * 8, 8), 8), :]
    x_far(3)
    a_pass((2, 2), (1, 3), 1)

    arrive(recv3.at[pl.ds(0, 15)], e_recv.at[5])
    total = recv3[0]
    for s in range(1, 16):
        total = total + recv3[s]
    fin[c] = total
    copy3f().start()
    a_pass((2, 3), (3, 1), 1)

    arrive(fin.at[1 - c], e_recv.at[6])
    for h in range(2):
        score_o[:, h * 256:(h + 1) * 256] = jnp.where(c == 0, fin[h, :4], fin[h, 4:])
    a_pass((3, 2), (3, 3), 2)

    for copy in sent:
        copy.wait_send()
    done_sending(8, copy1)
    done_sending(8, copy1b)
    done_sending(16, copy2)
    copy2c().wait_send()
    copy3c().wait_send()
    done_sending(16, copy3)
    copy3f().wait_send()

    def wrote(t, _):
        rows = pl.ds(pl.multiple_of(t * ROWS, ROWS), ROWS)
        pltpu.make_async_copy(act_v.at[rows], act_o.at[rows], out_sem.at[t]).wait()
        return 0

    lax.fori_loop(0, acc.shape[0] // ROWS, wrote, 0)


def per_device(acts, cotangent, out_weight, proj_in, proj_out, panels):
    rows, wide = cotangent.shape
    feats = acts.shape[1]
    any_spec = pl.BlockSpec(memory_space=pl.ANY)
    vmem_spec = pl.BlockSpec(memory_space=pltpu.VMEM)
    dma = pltpu.SemaphoreType.DMA
    return pl.pallas_call(
        kernel,
        out_shape=(
            jax.ShapeDtypeStruct((rows, feats), BF16),
            jax.ShapeDtypeStruct((128, 512), F32),
            jax.ShapeDtypeStruct((4, 512), F32),
        ),
        in_specs=[any_spec] * 6,
        out_specs=(any_spec, vmem_spec, vmem_spec),
        scratch_shapes=[
            pltpu.VMEM((rows, feats), BF16),
            pltpu.VMEM((rows, wide), BF16),
            pltpu.VMEM((feats, 128), BF16),
            pltpu.VMEM((64, feats), BF16),
            pltpu.VMEM((64, wide), BF16),
            pltpu.VMEM((128, 512), BF16),
            pltpu.VMEM((wide, feats), BF16),
            pltpu.VMEM((rows, feats), F32),
            pltpu.VMEM((rows, feats), BF16),
            pltpu.VMEM((4, 32, 128), F32),
            pltpu.VMEM((8, 16, 128), F32),
            pltpu.VMEM((8, 16, 128), F32),
            pltpu.VMEM((16, 128), BF16),
            pltpu.VMEM((8, 16, 128), BF16),
            pltpu.VMEM((16, 2, 16, 128), BF16),
            pltpu.VMEM((2, 16, 2, 16, 128), BF16),
            pltpu.VMEM((2, 128, 256), F32),
            pltpu.VMEM((128, 256), F32),
            pltpu.VMEM((128, 256), F32),
            pltpu.VMEM((16, 8, 256), F32),
            pltpu.VMEM((2, 8, 256), F32),
            dma((5,)),
            dma((4,)),
            dma((rows // ROWS,)),
            dma((36,)),
            dma((4,)),
            dma((4, 4)),
            dma((4, 4)),
            dma((7, 16)),
            dma((7,)),
        ],
        compiler_params=pltpu.CompilerParams(
            collective_id=0, has_side_effects=True, vmem_limit_bytes=60 * 1024 * 1024
        ),
        cost_estimate=pl.CostEstimate(
            flops=2 * rows * wide * (feats + 64), bytes_accessed=26 * 2**20, transcendentals=0
        ),
    )(acts, cotangent, out_weight, proj_in.T, proj_out.T, panels)


def solution(mesh):
    return jax.shard_map(
        per_device,
        mesh=mesh,
        in_specs=(
            P("dp", "fisher"),
            P("dp", None),
            P("fisher", "dp"),
            P("fisher", None),
            P(),
            P("dp", "fisher"),
        ),
        out_specs=(P("dp", "fisher"), P("dp", "fisher"), P("dp", "fisher")),
        check_vma=False,
    )
```

```python
import functools
import math

import jax
import jax.numpy as jnp
from jax import lax
from jax.experimental import pallas as pl
from jax.experimental.pallas import tpu as pltpu
from jax.sharding import PartitionSpec as P

LEN = 512
MESH = pl.DeviceIdType.MESH
F32 = jnp.float32
BF16 = jnp.bfloat16
PIECE = 256


def dot(a, b, ca=1, cb=0, precision=None):
    return lax.dot_general(
        a, b, (((ca,), (cb,)), ((), ())), preferred_element_type=F32, precision=precision
    )


def two_parts(v):
    high = v.astype(BF16)
    return jnp.concatenate([high, (v - high.astype(F32)).astype(BF16)], axis=1)


def kernel(
    acts_h, cot_h, w_h, pin_h, pout_h, pan_h,
    act_o, fish_o, score_o,
    acts, cot, w_own, pin, pout, pan, wg, acc,
    in_send, in_recv, q_part, q_all, tiles_f, tiles, send2, g_all, s_part, s_recv,
    in_sem, cot_sem,
    w_send, rz, rx, rsib,
    e_send, e_recv,
):
    i = lax.axis_index("dp")
    j = lax.axis_index("fisher")
    c = lax.rem(i, 2)
    q = i // 2
    zh = lax.rem(q, 4)
    x = q // 4
    sib = (i + 1 - 2 * c, j)

    def chip(dx, dz):
        return lax.rem(x + dx + 4, 4) * 4 + lax.rem(zh + dz + 4, 4)

    def dev(dx, dz):
        return (chip(dx, dz) * 2 + c, j)

    loads = [
        pltpu.make_async_copy(w_h, w_own, in_sem.at[0]),
        pltpu.make_async_copy(acts_h, acts, in_sem.at[1]),
        pltpu.make_async_copy(pin_h, pin, in_sem.at[2]),
        pltpu.make_async_copy(pout_h, pout, in_sem.at[3]),
        pltpu.make_async_copy(pan_h, pan.at[c], in_sem.at[4]),
    ]

    def cot_load(s):
        rows = pl.ds(pl.multiple_of(lax.rem(j + s, 8) * PIECE, PIECE), PIECE)
        return pltpu.make_async_copy(cot_h.at[rows], cot.at[rows], cot_sem.at[s])

    for load in loads:
        load.start()
    cot_load(0).start()

    barrier = pltpu.get_barrier_semaphore()
    pl.semaphore_signal(barrier, inc=1, device_id=sib, device_id_type=MESH)

    @pl.loop(1, 8)
    def _(s):
        pl.semaphore_signal(barrier, inc=1, device_id=(i, lax.rem(j + s, 8)), device_id_type=MESH)

    @pl.loop(1, 16)
    def _(s):
        pl.semaphore_signal(
            barrier, inc=1, device_id=(lax.rem(q + s, 16) * 2 + c, j), device_id_type=MESH
        )

    eye = jnp.where(
        lax.broadcasted_iota(jnp.int32, (128, 128), 0) == lax.broadcasted_iota(jnp.int32, (128, 128), 1),
        1.0, 0.0,
    ).astype(BF16)
    loads[0].wait()
    wg[pl.ds(pl.multiple_of(q * 256 + c * 128, 128), 128), :] = dot(eye, w_own[...], 1, 1).astype(BF16)

    loads[1].wait()
    loads[2].wait()
    ip = dot(acts[...], pin[...], 1, 1)
    for to in range(8):
        block = ip[to * PIECE:(to + 1) * PIECE]
        in_send[to] = jnp.concatenate([block[:128], block[128:]], axis=1)
    loads[4].wait()
    pl.semaphore_wait(barrier, 23)

    def remote(src, dst, to, stage, s=0):
        return pltpu.make_async_remote_copy(
            src_ref=src, dst_ref=dst, send_sem=e_send.at[stage, s], recv_sem=e_recv.at[stage],
            device_id=to, device_id_type=MESH,
        )

    def copy_in(s):
        to = lax.rem(j + s, 8)
        return remote(in_send.at[to], in_recv.at[j], (i, to), 0, s)

    def copy_part(s):
        return remote(q_part, q_all.at[j], (i, lax.rem(j + s, 8)), 1, s)

    def copy_grads(s):
        to = lax.rem(q + s, 16)
        return remote(send2.at[to], g_all.at[c, q], (to * 2 + c, j), 2, s)

    def copy_pair():
        return remote(g_all.at[c], g_all.at[c], sib, 3)

    def copy_scores(s):
        to = lax.rem(q + s, 16)
        return remote(s_part.at[to], s_recv.at[q], (to * 2 + c, j), 4, s)

    def copy_panels():
        return remote(pan.at[c], pan.at[c], sib, 5)

    def exchange(n, copy_of):
        def go(s, _):
            copy_of(s).start()
            return 0
        lax.fori_loop(1, n, go, 0)

    def done_sending(n, copy_of):
        def go(s, _):
            copy_of(s).wait_send()
            return 0
        lax.fori_loop(1, n, go, 0)

    exchange(8, copy_in)
    copy_panels().start()

    def wrows(chip_index, core, half=None):
        start = chip_index * 256 + core * 128
        if half is None:
            return wg.at[pl.ds(pl.multiple_of(start, 128), 128)]
        return wg.at[pl.ds(pl.multiple_of(start + 64 * half, 64), 64)]

    sent = []

    def push(ref, to, recv):
        copy = pltpu.make_async_remote_copy(
            src_ref=ref, dst_ref=ref, send_sem=w_send.at[len(sent)], recv_sem=recv,
            device_id=to, device_id_type=MESH,
        )
        copy.start()
        sent.append(copy)

    def arrive(ref, sem):
        pltpu.make_async_copy(ref, ref, sem).wait()

    DZ = (0, -1, 1, 2)
    DX = (0, -1, 1, 2)

    def to_x(m):
        push(wrows(chip(0, DZ[m]), c), dev(1, 0), rx.at[m, 0])
        push(wrows(chip(0, DZ[m]), c), dev(-1, 0), rx.at[m, 1])

    def to_sib(m, k):
        push(wrows(chip(DX[k], DZ[m]), c), sib, rsib.at[m, k])

    push(wrows(q, c), dev(0, 1), rz.at[0])
    push(wrows(q, c), dev(0, -1), rz.at[1])
    to_x(0)
    to_sib(0, 0)

    def x_near(m):
        arrive(wrows(chip(-1, DZ[m]), c), rx.at[m, 0])
        push(wrows(chip(-1, DZ[m]), c, 0), dev(1, 0), rx.at[m, 2])
        to_sib(m, 1)
        arrive(wrows(chip(1, DZ[m]), c), rx.at[m, 1])
        push(wrows(chip(1, DZ[m]), c, 1), dev(-1, 0), rx.at[m, 3])
        to_sib(m, 2)

    def x_far(m):
        arrive(wrows(chip(2, DZ[m]), c, 0), rx.at[m, 2])
        arrive(wrows(chip(2, DZ[m]), c, 1), rx.at[m, 3])
        to_sib(m, 3)

    def z_near():
        arrive(wrows(chip(0, -1), c), rz.at[0])
        push(wrows(chip(0, -1), c, 0), dev(0, 1), rz.at[2])
        to_x(1)
        arrive(wrows(chip(0, 1), c), rz.at[1])
        push(wrows(chip(0, 1), c, 1), dev(0, -1), rz.at[3])
        to_x(2)
        to_sib(1, 0)
        to_sib(2, 0)

    def z_far():
        arrive(wrows(chip(0, 2), c, 0), rz.at[2])
        arrive(wrows(chip(0, 2), c, 1), rz.at[3])
        to_x(3)
        to_sib(3, 0)

    for step in range(1, 8):
        cot_load(step).start()

    loads[3].wait()
    row = lax.broadcasted_iota(jnp.int32, (64, 64), 0)
    col = lax.broadcasted_iota(jnp.int32, (64, 64), 1)
    even_odd = jnp.where(col == lax.rem(row, 32) * 2 + row // 32, 1.0, 0.0).astype(BF16)
    pout[...] = dot(even_odd, pout[...]).astype(BF16)
    cot_load(0).wait()
    op = dot(cot[pl.ds(pl.multiple_of(j * PIECE, PIECE), PIECE), :], pout[...], 1, 1)
    op_parts = two_parts(jnp.concatenate([op[:128], op[128:]], axis=1))

    def a_pass(first, second, mode):
        for m, k in (first, second):
            arrive(wrows(chip(DX[k], DZ[m]), 1 - c), rsib.at[m, k])
        ka = pl.ds(pl.multiple_of(chip(DX[first[1]], DZ[first[0]]) * 256, 256), 256)
        kb = pl.ds(pl.multiple_of(chip(DX[second[1]], DZ[second[0]]) * 256, 256), 256)
        new = dot(cot[:, ka], wg[ka, :]) + dot(cot[:, kb], wg[kb, :])
        if mode == 0:
            acc[...] = new
        elif mode == 1:
            acc[...] += new
        else:
            act_o[...] = (acc[...] + new).astype(BF16)

    x_near(0)
    for step in range(1, 8):
        cot_load(step).wait()
    a_pass((0, 0), (0, 1), 0)
    z_near()
    x_far(0)

    arrive(in_recv.at[pl.ds(0, 7)], e_recv.at[0])
    total = in_send[j]
    for step in range(1, 8):
        total = total + in_recv[lax.rem(j + step, 8)]
    part = dot(op_parts, two_parts(total), 0, 0)
    part = (part[:128, :128] + part[128:, 128:]) + (part[:128, 128:] + part[128:, :128])
    part = part[:64, :64] + part[64:, 64:]
    part = jnp.concatenate([part[:32], part[32:]], axis=1)
    q_part[...] = part
    exchange(8, copy_part)
    q_all[j] = part
    a_pass((0, 2), (1, 0), 1)
    z_far()
    a_pass((2, 0), (0, 3), 1)
    x_near(1)
    x_near(2)

    arrive(q_all.at[pl.ds(0, 7)], e_recv.at[1])
    for e in range(4):
        grads = (q_all[2 * e] + q_all[2 * e + 1]) * (1.0 / math.sqrt(LEN))
        for t in range(8):
            tiles_f[t, e * 4:e * 4 + 4, :] = grads[t * 4:t * 4 + 4]
    tiles[...] = tiles_f[...].astype(BF16)
    mine = tiles[j]
    for to in range(16):
        send2[to, 0] = tiles[to // 2]
        send2[to, 1] = mine
    exchange(16, copy_grads)
    g_all[c, q] = send2[q]
    a_pass((3, 0), (1, 1), 1)
    x_near(3)
    a_pass((1, 2), (2, 1), 1)
    x_far(1)
    x_far(2)
    a_pass((2, 2), (1, 3), 1)
    x_far(3)

    m = lax.broadcasted_iota(jnp.int32, (64, 256), 0)
    n = lax.broadcasted_iota(jnp.int32, (64, 256), 1)
    pick = [jnp.where(n == m * 4 + lax.rem(q, 2) * 2 + u, 1.0, 0.0).astype(BF16) for u in range(2)]
    arrive(pan.at[1 - c], e_recv.at[5])
    arrive(g_all.at[c, pl.ds(0, 15)], e_recv.at[2])
    copy_pair().start()
    own_tiles = g_all[c, :, 0].reshape(256, 128)
    score = dot(dot(pick[0], own_tiles).astype(BF16), pan[0])
    score += dot(dot(pick[1], own_tiles).astype(BF16), pan[1])
    for to in range(16):
        s_part[to] = score[to * 4:to * 4 + 4]
    exchange(16, copy_scores)
    a_pass((2, 3), (3, 1), 1)

    arrive(g_all.at[1 - c], e_recv.at[3])
    m = lax.broadcasted_iota(jnp.int32, (128, 512), 0)
    n = lax.broadcasted_iota(jnp.int32, (128, 512), 1)

    def select(r):
        return jnp.where(n == m * 4 + r, 1.0, 0.0).astype(BF16)

    row_tiles = g_all[:, :, 0].reshape(512, 128)
    col_tiles = g_all[:, :, 1].reshape(512, 128)
    g_rows = dot(select(lax.rem(i, 4)), row_tiles).astype(BF16)
    g_cols = jnp.concatenate([dot(select(r), col_tiles).astype(BF16) for r in range(4)], axis=1)
    fish_o[...] = dot(g_rows, g_cols, 0, 0) * (1.0 / 128)
    a_pass((3, 2), (3, 3), 2)

    arrive(s_recv.at[pl.ds(0, 15)], e_recv.at[4])
    total = s_part[q]
    for step in range(1, 16):
        total = total + s_recv[lax.rem(q + step, 16)]
    score_o[...] = total

    for copy in sent:
        copy.wait_send()
    done_sending(8, copy_in)
    done_sending(8, copy_part)
    done_sending(16, copy_grads)
    done_sending(16, copy_scores)
    copy_pair().wait_send()
    copy_panels().wait_send()


def per_device(acts, cotangent, out_weight, proj_in, proj_out, panels):
    rows, wide = cotangent.shape
    feats = acts.shape[1]
    any_spec = pl.BlockSpec(memory_space=pl.ANY)
    vmem_spec = pl.BlockSpec(memory_space=pltpu.VMEM)
    dma = pltpu.SemaphoreType.DMA
    operands = (acts, cotangent, out_weight, proj_in.T, proj_out.T, panels)
    operands = [pltpu.with_memory_space_constraint(a, pltpu.HBM) for a in operands]
    return pl.pallas_call(
        kernel,
        out_shape=(
            jax.ShapeDtypeStruct((rows, feats), BF16),
            jax.ShapeDtypeStruct((128, 512), F32),
            jax.ShapeDtypeStruct((4, 512), F32),
        ),
        in_specs=[any_spec] * 6,
        out_specs=(vmem_spec, vmem_spec, vmem_spec),
        scratch_shapes=[
            pltpu.VMEM((rows, feats), BF16),
            pltpu.VMEM((rows, wide), BF16),
            pltpu.VMEM((feats, 128), BF16),
            pltpu.VMEM((64, feats), BF16),
            pltpu.VMEM((64, wide), BF16),
            pltpu.VMEM((2, 128, 512), BF16),
            pltpu.VMEM((wide, feats), BF16),
            pltpu.VMEM((rows, feats), F32),
            pltpu.VMEM((8, 128, 128), F32),
            pltpu.VMEM((8, 128, 128), F32),
            pltpu.VMEM((32, 128), F32),
            pltpu.VMEM((8, 32, 128), F32),
            pltpu.VMEM((8, 16, 128), F32),
            pltpu.VMEM((8, 16, 128), BF16),
            pltpu.VMEM((16, 2, 16, 128), BF16),
            pltpu.VMEM((2, 16, 2, 16, 128), BF16),
            pltpu.VMEM((16, 4, 512), F32),
            pltpu.VMEM((16, 4, 512), F32),
            dma((5,)),
            dma((8,)),
            dma((36,)),
            dma((4,)),
            dma((4, 4)),
            dma((4, 4)),
            dma((6, 16)),
            dma((6,)),
        ],
        compiler_params=pltpu.CompilerParams(
            collective_id=0, has_side_effects=True, vmem_limit_bytes=40 * 1024 * 1024
        ),
        cost_estimate=pl.CostEstimate(
            flops=2 * rows * wide * (feats + 64), bytes_accessed=26 * 2**20, transcendentals=0
        ),
    )(*operands)


def solution(mesh):
    return jax.shard_map(
        per_device,
        mesh=mesh,
        in_specs=(
            P("dp", "fisher"),
            P("dp", None),
            P("fisher", "dp"),
            P("fisher", None),
            P(),
            P("dp", "fisher"),
        ),
        out_specs=(P("dp", "fisher"), P("dp", "fisher"), P("dp", "fisher")),
        check_vma=False,
    )
```

```python
import functools
import math

import jax
import jax.numpy as jnp
from jax import lax
from jax.experimental import pallas as pl
from jax.experimental.pallas import tpu as pltpu
from jax.sharding import PartitionSpec as P

LEN = 512
MESH = pl.DeviceIdType.MESH
F32 = jnp.float32
BF16 = jnp.bfloat16
PIECE = 256


def dot(a, b, ca=1, cb=0, precision=None):
    return lax.dot_general(
        a, b, (((ca,), (cb,)), ((), ())), preferred_element_type=F32, precision=precision
    )


def two_parts(v):
    high = v.astype(BF16)
    return jnp.concatenate([high, (v - high.astype(F32)).astype(BF16)], axis=1)


def kernel(
    acts_h, cot_h, w_h, pin_h, pout_h, pan_h,
    act_o, fish_o, score_o,
    acts, cot, w_own, pin, pout, pan, wg, acc,
    in_send, in_recv, q_part, q_all, tiles_f, tiles, g_rows_all, g_cols_all, s_part, s_recv,
    in_sem, cot_sem,
    w_send, rz, rx, rsib,
    e_send, e_recv,
):
    i = lax.axis_index("dp")
    j = lax.axis_index("fisher")
    c = lax.rem(i, 2)
    q = i // 2
    zh = lax.rem(q, 4)
    x = q // 4
    sib = (i + 1 - 2 * c, j)

    def chip(dx, dz):
        return lax.rem(x + dx + 4, 4) * 4 + lax.rem(zh + dz + 4, 4)

    def dev(dx, dz):
        return (chip(dx, dz) * 2 + c, j)

    loads = [
        pltpu.make_async_copy(w_h, w_own, in_sem.at[0]),
        pltpu.make_async_copy(acts_h, acts, in_sem.at[1]),
        pltpu.make_async_copy(pin_h, pin, in_sem.at[2]),
        pltpu.make_async_copy(pout_h, pout, in_sem.at[3]),
        pltpu.make_async_copy(pan_h, pan.at[c], in_sem.at[4]),
    ]

    def cot_load(s):
        rows = pl.ds(pl.multiple_of(lax.rem(j + s, 8) * PIECE, PIECE), PIECE)
        return pltpu.make_async_copy(cot_h.at[rows], cot.at[rows], cot_sem.at[s])

    for load in loads:
        load.start()
    cot_load(0).start()

    barrier = pltpu.get_barrier_semaphore()
    pl.semaphore_signal(barrier, inc=1, device_id=sib, device_id_type=MESH)

    @pl.loop(1, 8)
    def _(s):
        pl.semaphore_signal(barrier, inc=1, device_id=(i, lax.rem(j + s, 8)), device_id_type=MESH)

    @pl.loop(1, 16)
    def _(s):
        pl.semaphore_signal(
            barrier, inc=1, device_id=(lax.rem(q + s, 16) * 2 + c, j), device_id_type=MESH
        )

    eye = jnp.where(
        lax.broadcasted_iota(jnp.int32, (128, 128), 0) == lax.broadcasted_iota(jnp.int32, (128, 128), 1),
        1.0, 0.0,
    ).astype(BF16)
    loads[0].wait()
    wg[pl.ds(pl.multiple_of(q * 256 + c * 128, 128), 128), :] = dot(eye, w_own[...], 1, 1).astype(BF16)

    loads[1].wait()
    loads[2].wait()
    ip = dot(acts[...], pin[...], 1, 1)
    for to in range(8):
        block = ip[to * PIECE:(to + 1) * PIECE]
        in_send[to] = jnp.concatenate([block[:128], block[128:]], axis=1).astype(BF16)
    loads[4].wait()
    pl.semaphore_wait(barrier, 23)

    def remote(src, dst, to, stage, s=0):
        return pltpu.make_async_remote_copy(
            src_ref=src, dst_ref=dst, send_sem=e_send.at[stage, s], recv_sem=e_recv.at[stage],
            device_id=to, device_id_type=MESH,
        )

    def copy_in(s):
        to = lax.rem(j + s, 8)
        return remote(in_send.at[to], in_recv.at[j], (i, to), 0, s)

    def copy_part(s):
        return remote(q_part, q_all.at[j], (i, lax.rem(j + s, 8)), 1, s)

    def copy_grads(s):
        to = lax.rem(q + s, 16)
        return remote(tiles.at[to // 2], g_rows_all.at[c, q], (to * 2 + c, j), 2, s)

    def copy_cols(s):
        to = lax.rem(q + s, 16)
        return remote(tiles.at[j], g_cols_all.at[c, q], (to * 2 + c, j), 6, s)

    def copy_pair():
        return remote(g_rows_all.at[c], g_rows_all.at[c], sib, 3)

    def copy_pair_cols():
        return remote(g_cols_all.at[c], g_cols_all.at[c], sib, 7)

    def copy_scores(s):
        to = lax.rem(q + s, 16)
        return remote(s_part.at[to], s_recv.at[q], (to * 2 + c, j), 4, s)

    def copy_panels():
        return remote(pan.at[c], pan.at[c], sib, 5)

    def exchange(n, copy_of):
        def go(s, _):
            copy_of(s).start()
            return 0
        lax.fori_loop(1, n, go, 0)

    def done_sending(n, copy_of):
        def go(s, _):
            copy_of(s).wait_send()
            return 0
        lax.fori_loop(1, n, go, 0)

    exchange(8, copy_in)
    copy_panels().start()

    def wrows(chip_index, core, half=None):
        start = chip_index * 256 + core * 128
        if half is None:
            return wg.at[pl.ds(pl.multiple_of(start, 128), 128)]
        return wg.at[pl.ds(pl.multiple_of(start + 64 * half, 64), 64)]

    sent = []

    def push(ref, to, recv):
        copy = pltpu.make_async_remote_copy(
            src_ref=ref, dst_ref=ref, send_sem=w_send.at[len(sent)], recv_sem=recv,
            device_id=to, device_id_type=MESH,
        )
        copy.start()
        sent.append(copy)

    def arrive(ref, sem):
        pltpu.make_async_copy(ref, ref, sem).wait()

    DZ = (0, -1, 1, 2)
    DX = (0, -1, 1, 2)

    def to_x(m, h):
        block = wrows(chip(0, DZ[m]), c, h)
        if h == 0:
            push(block, dev(1, 0), rx.at[m, 0, h])
            push(block, dev(-1, 0), rx.at[m, 1, h])
        else:
            push(block, dev(-1, 0), rx.at[m, 1, h])
            push(block, dev(1, 0), rx.at[m, 0, h])

    def to_sib(m, k):
        push(wrows(chip(DX[k], DZ[m]), c), sib, rsib.at[m, k])

    push(wrows(q, c, 0), dev(0, 1), rz.at[0, 0])
    push(wrows(q, c, 1), dev(0, -1), rz.at[1, 1])
    push(wrows(q, c, 0), dev(1, 0), rx.at[0, 0, 0])
    push(wrows(q, c, 1), dev(-1, 0), rx.at[0, 1, 1])
    push(wrows(q, c, 1), dev(0, 1), rz.at[0, 1])
    push(wrows(q, c, 0), dev(0, -1), rz.at[1, 0])
    push(wrows(q, c, 1), dev(1, 0), rx.at[0, 0, 1])
    push(wrows(q, c, 0), dev(-1, 0), rx.at[0, 1, 0])
    to_sib(0, 0)

    def x_up(m):
        block = wrows(chip(-1, DZ[m]), c, 0)
        arrive(block, rx.at[m, 0, 0])
        push(block, dev(1, 0), rx.at[m, 2, 0])

    def x_down(m):
        block = wrows(chip(1, DZ[m]), c, 1)
        arrive(block, rx.at[m, 1, 1])
        push(block, dev(-1, 0), rx.at[m, 2, 1])

    def x_rest(m):
        arrive(wrows(chip(-1, DZ[m]), c, 1), rx.at[m, 0, 1])
        to_sib(m, 1)
        arrive(wrows(chip(1, DZ[m]), c, 0), rx.at[m, 1, 0])
        to_sib(m, 2)

    def x_far(m):
        arrive(wrows(chip(2, DZ[m]), c, 0), rx.at[m, 2, 0])
        arrive(wrows(chip(2, DZ[m]), c, 1), rx.at[m, 2, 1])
        to_sib(m, 3)

    def z_first():
        arrive(wrows(chip(0, -1), c, 0), rz.at[0, 0])
        push(wrows(chip(0, -1), c, 0), dev(0, 1), rz.at[2, 0])
        to_x(1, 0)
        arrive(wrows(chip(0, 1), c, 1), rz.at[1, 1])
        push(wrows(chip(0, 1), c, 1), dev(0, -1), rz.at[2, 1])
        to_x(2, 1)

    def z_rest():
        arrive(wrows(chip(0, -1), c, 1), rz.at[0, 1])
        to_x(1, 1)
        arrive(wrows(chip(0, 1), c, 0), rz.at[1, 0])
        to_x(2, 0)
        to_sib(1, 0)
        to_sib(2, 0)

    def z_far():
        arrive(wrows(chip(0, 2), c, 0), rz.at[2, 0])
        to_x(3, 0)
        arrive(wrows(chip(0, 2), c, 1), rz.at[2, 1])
        to_x(3, 1)
        to_sib(3, 0)

    for step in range(1, 8):
        cot_load(step).start()

    loads[3].wait()
    row = lax.broadcasted_iota(jnp.int32, (64, 64), 0)
    col = lax.broadcasted_iota(jnp.int32, (64, 64), 1)
    even_odd = jnp.where(col == lax.rem(row, 32) * 2 + row // 32, 1.0, 0.0).astype(BF16)
    pout[...] = dot(even_odd, pout[...]).astype(BF16)
    cot_load(0).wait()
    op = dot(cot[pl.ds(pl.multiple_of(j * PIECE, PIECE), PIECE), :], pout[...], 1, 1)
    op_parts = two_parts(jnp.concatenate([op[:128], op[128:]], axis=1))

    def a_pass(first, second, mode):
        for m, k in (first, second):
            arrive(wrows(chip(DX[k], DZ[m]), 1 - c), rsib.at[m, k])
        ka = pl.ds(pl.multiple_of(chip(DX[first[1]], DZ[first[0]]) * 256, 256), 256)
        kb = pl.ds(pl.multiple_of(chip(DX[second[1]], DZ[second[0]]) * 256, 256), 256)
        new = dot(cot[:, ka], wg[ka, :]) + dot(cot[:, kb], wg[kb, :])
        if mode == 0:
            acc[...] = new
        elif mode == 1:
            acc[...] += new
        else:
            act_o[...] = (acc[...] + new).astype(BF16)

    x_up(0)
    x_down(0)
    x_rest(0)
    z_first()

    arrive(in_recv.at[pl.ds(0, 7)], e_recv.at[0])
    total = in_send[j].astype(F32)
    for step in range(1, 8):
        total = total + in_recv[lax.rem(j + step, 8)].astype(F32)
    part = dot(op_parts, two_parts(total), 0, 0)
    part = (part[:128, :128] + part[128:, 128:]) + (part[:128, 128:] + part[128:, :128])
    part = part[:64, :64] + part[64:, 64:]
    part = jnp.concatenate([part[:32], part[32:]], axis=1)
    q_part[...] = part
    exchange(8, copy_part)
    q_all[j] = part
    for step in range(1, 8):
        cot_load(step).wait()
    a_pass((0, 0), (0, 1), 0)
    x_far(0)
    z_rest()
    x_up(1)
    x_down(2)
    a_pass((0, 2), (1, 0), 1)

    arrive(q_all.at[pl.ds(0, 7)], e_recv.at[1])
    for e in range(4):
        grads = (q_all[2 * e] + q_all[2 * e + 1]) * (1.0 / math.sqrt(LEN))
        for t in range(8):
            tiles_f[t, e * 4:e * 4 + 4, :] = grads[t * 4:t * 4 + 4]
    tiles[...] = tiles_f[...].astype(BF16)
    exchange(16, copy_grads)
    exchange(16, copy_cols)
    g_rows_all[c, q] = tiles[q // 2]
    g_cols_all[c, q] = tiles[j]
    z_far()
    x_down(1)
    x_up(2)
    a_pass((2, 0), (0, 3), 1)
    x_rest(1)
    x_rest(2)
    a_pass((3, 0), (1, 1), 1)

    m = lax.broadcasted_iota(jnp.int32, (64, 256), 0)
    n = lax.broadcasted_iota(jnp.int32, (64, 256), 1)
    pick = [jnp.where(n == m * 4 + lax.rem(q, 2) * 2 + u, 1.0, 0.0).astype(BF16) for u in range(2)]
    arrive(pan.at[1 - c], e_recv.at[5])
    arrive(g_rows_all.at[c, pl.ds(0, 15)], e_recv.at[2])
    own_tiles = g_rows_all[c].reshape(256, 128)
    score = dot(dot(pick[0], own_tiles).astype(BF16), pan[0])
    score += dot(dot(pick[1], own_tiles).astype(BF16), pan[1])
    for to in range(16):
        s_part[to] = score[to * 4:to * 4 + 4]
    exchange(16, copy_scores)
    x_up(3)
    x_down(3)
    copy_pair().start()
    arrive(g_cols_all.at[c, pl.ds(0, 15)], e_recv.at[6])
    copy_pair_cols().start()
    x_far(1)
    x_far(2)
    a_pass((1, 2), (2, 1), 1)
    x_rest(3)
    a_pass((2, 2), (1, 3), 1)
    x_far(3)
    a_pass((2, 3), (3, 1), 1)

    arrive(g_rows_all.at[1 - c], e_recv.at[3])
    arrive(g_cols_all.at[1 - c], e_recv.at[7])
    m = lax.broadcasted_iota(jnp.int32, (128, 512), 0)
    n = lax.broadcasted_iota(jnp.int32, (128, 512), 1)

    def select(r):
        return jnp.where(n == m * 4 + r, 1.0, 0.0).astype(BF16)

    row_tiles = g_rows_all[...].reshape(512, 128)
    col_tiles = g_cols_all[...].reshape(512, 128)
    g_rows = dot(select(lax.rem(i, 4)), row_tiles).astype(BF16)
    g_cols = jnp.concatenate([dot(select(r), col_tiles).astype(BF16) for r in range(4)], axis=1)
    fish_o[...] = dot(g_rows, g_cols, 0, 0) * (1.0 / 128)
    a_pass((3, 2), (3, 3), 2)

    arrive(s_recv.at[pl.ds(0, 15)], e_recv.at[4])
    total = s_part[q]
    for step in range(1, 16):
        total = total + s_recv[lax.rem(q + step, 16)]
    score_o[...] = total

    for copy in sent:
        copy.wait_send()
    done_sending(8, copy_in)
    done_sending(8, copy_part)
    done_sending(16, copy_grads)
    done_sending(16, copy_cols)
    copy_pair_cols().wait_send()
    done_sending(16, copy_scores)
    copy_pair().wait_send()
    copy_panels().wait_send()


def per_device(acts, cotangent, out_weight, proj_in, proj_out, panels):
    rows, wide = cotangent.shape
    feats = acts.shape[1]
    any_spec = pl.BlockSpec(memory_space=pl.ANY)
    vmem_spec = pl.BlockSpec(memory_space=pltpu.VMEM)
    dma = pltpu.SemaphoreType.DMA
    operands = (acts, cotangent, out_weight, proj_in.T, proj_out.T, panels)
    operands = [pltpu.with_memory_space_constraint(a, pltpu.HBM) for a in operands]
    return pl.pallas_call(
        kernel,
        out_shape=(
            jax.ShapeDtypeStruct((rows, feats), BF16),
            jax.ShapeDtypeStruct((128, 512), F32),
            jax.ShapeDtypeStruct((4, 512), F32),
        ),
        in_specs=[any_spec] * 6,
        out_specs=(vmem_spec, vmem_spec, vmem_spec),
        scratch_shapes=[
            pltpu.VMEM((rows, feats), BF16),
            pltpu.VMEM((rows, wide), BF16),
            pltpu.VMEM((feats, 128), BF16),
            pltpu.VMEM((64, feats), BF16),
            pltpu.VMEM((64, wide), BF16),
            pltpu.VMEM((2, 128, 512), BF16),
            pltpu.VMEM((wide, feats), BF16),
            pltpu.VMEM((rows, feats), F32),
            pltpu.VMEM((8, 128, 128), BF16),
            pltpu.VMEM((8, 128, 128), BF16),
            pltpu.VMEM((32, 128), F32),
            pltpu.VMEM((8, 32, 128), F32),
            pltpu.VMEM((8, 16, 128), F32),
            pltpu.VMEM((8, 16, 128), BF16),
            pltpu.VMEM((2, 16, 16, 128), BF16),
            pltpu.VMEM((2, 16, 16, 128), BF16),
            pltpu.VMEM((16, 4, 512), F32),
            pltpu.VMEM((16, 4, 512), F32),
            dma((5,)),
            dma((8,)),
            dma((46,)),
            dma((3, 2)),
            dma((4, 3, 2)),
            dma((4, 4)),
            dma((8, 16)),
            dma((8,)),
        ],
        compiler_params=pltpu.CompilerParams(
            collective_id=0, has_side_effects=True, vmem_limit_bytes=40 * 1024 * 1024
        ),
        cost_estimate=pl.CostEstimate(
            flops=2 * rows * wide * (feats + 64), bytes_accessed=26 * 2**20, transcendentals=0
        ),
    )(*operands)


def solution(mesh):
    return jax.shard_map(
        per_device,
        mesh=mesh,
        in_specs=(
            P("dp", "fisher"),
            P("dp", None),
            P("fisher", "dp"),
            P("fisher", None),
            P(),
            P("dp", "fisher"),
        ),
        out_specs=(P("dp", "fisher"), P("dp", "fisher"), P("dp", "fisher")),
        check_vma=False,
    )
```

```python
import functools
import math

import jax
import jax.numpy as jnp
from jax import lax
from jax.experimental import pallas as pl
from jax.experimental.pallas import tpu as pltpu
from jax.sharding import PartitionSpec as P

LEN = 512
MESH = pl.DeviceIdType.MESH
F32 = jnp.float32
BF16 = jnp.bfloat16
PIECE = 256


def dot(a, b, ca=1, cb=0, precision=None):
    return lax.dot_general(
        a, b, (((ca,), (cb,)), ((), ())), preferred_element_type=F32, precision=precision
    )


def two_parts(v):
    high = v.astype(BF16)
    return jnp.concatenate([high, (v - high.astype(F32)).astype(BF16)], axis=1)


def kernel(
    acts_h, cot_h, w_h, pin_h, pout_h, pan_h,
    act_o, fish_o, score_o,
    acts, cot, w_own, pin, pout, pan, wg, acc,
    in_send, in_recv, q_part, q_all, tiles_f, tiles, g_rows_all, g_cols_all, s_part, s_recv,
    in_sem, cot_sem,
    w_send, rz, rx, rsib,
    e_send, e_recv, word,
):
    i = lax.axis_index("dp")
    j = lax.axis_index("fisher")
    c = lax.rem(i, 2)
    q = i // 2
    zh = lax.rem(q, 4)
    x = q // 4
    sib = (i + 1 - 2 * c, j)

    def chip(dx, dz):
        return lax.rem(x + dx + 4, 4) * 4 + lax.rem(zh + dz + 4, 4)

    def dev(dx, dz):
        return (chip(dx, dz) * 2 + c, j)

    loads = [
        pltpu.make_async_copy(w_h, w_own, in_sem.at[0]),
        pltpu.make_async_copy(acts_h, acts, in_sem.at[1]),
        pltpu.make_async_copy(pin_h, pin, in_sem.at[2]),
        pltpu.make_async_copy(pout_h, pout, in_sem.at[3]),
        pltpu.make_async_copy(pan_h, pan.at[c], in_sem.at[4]),
    ]

    def cot_load(s):
        rows = pl.ds(pl.multiple_of(lax.rem(j + s, 8) * PIECE, PIECE), PIECE)
        return pltpu.make_async_copy(cot_h.at[rows], cot.at[rows], cot_sem.at[s])

    for load in loads[:3]:
        load.start()

    barrier = pltpu.get_barrier_semaphore()
    pl.semaphore_signal(barrier, inc=1, device_id=sib, device_id_type=MESH)

    @pl.loop(1, 8)
    def _(s):
        pl.semaphore_signal(barrier, inc=1, device_id=(i, lax.rem(j + s, 8)), device_id_type=MESH)

    for near in (dev(1, 0), dev(-1, 0), dev(0, 1), dev(0, -1)):
        pl.semaphore_signal(barrier, inc=1, device_id=near, device_id_type=MESH)

    for load in loads[3:]:
        load.start()
    cot_load(0).start()

    eye = jnp.where(
        lax.broadcasted_iota(jnp.int32, (128, 128), 0) == lax.broadcasted_iota(jnp.int32, (128, 128), 1),
        1.0, 0.0,
    ).astype(BF16)
    loads[0].wait()
    wg[pl.ds(pl.multiple_of(q * 256 + c * 128, 128), 128), :] = dot(eye, w_own[...], 1, 1).astype(BF16)

    pl.semaphore_wait(barrier, 12)

    def tell(k):
        for to in ((dev(1, 0), dev(-1, 0)) if k == 0 else (dev(0, 1), dev(0, -1))):
            pl.semaphore_signal(word.at[k], inc=1, device_id=to, device_id_type=MESH)

    def hear(k):
        pl.semaphore_wait(word.at[k], 2)

    tell(0)

    def remote(src, dst, to, stage, s=0):
        return pltpu.make_async_remote_copy(
            src_ref=src, dst_ref=dst, send_sem=e_send.at[stage, s], recv_sem=e_recv.at[stage],
            device_id=to, device_id_type=MESH,
        )

    def copy_in(s):
        to = lax.rem(j + s, 8)
        return remote(in_send.at[to], in_recv.at[j], (i, to), 0, s)

    def copy_part(s):
        return remote(q_part, q_all.at[j], (i, lax.rem(j + s, 8)), 1, s)

    def copy_grads(s):
        to = lax.rem(q + s, 16)
        return remote(tiles.at[to // 2], g_rows_all.at[c, q], (to * 2 + c, j), 2, s)

    def copy_cols(s):
        to = lax.rem(q + s, 16)
        return remote(tiles.at[j], g_cols_all.at[c, q], (to * 2 + c, j), 6, s)

    def copy_pair():
        return remote(g_rows_all.at[c], g_rows_all.at[c], sib, 3)

    def copy_pair_cols():
        return remote(g_cols_all.at[c], g_cols_all.at[c], sib, 7)

    def copy_scores(s):
        to = lax.rem(q + s, 16)
        return remote(s_part.at[to], s_recv.at[q], (to * 2 + c, j), 4, s)

    def copy_panels():
        return remote(pan.at[c], pan.at[c], sib, 5)

    def exchange(n, copy_of):
        def go(s, _):
            copy_of(s).start()
            return 0
        lax.fori_loop(1, n, go, 0)

    def done_sending(n, copy_of):
        def go(s, _):
            copy_of(s).wait_send()
            return 0
        lax.fori_loop(1, n, go, 0)

    def wrows(chip_index, core, half=None):
        start = chip_index * 256 + core * 128
        if half is None:
            return wg.at[pl.ds(pl.multiple_of(start, 128), 128)]
        return wg.at[pl.ds(pl.multiple_of(start + 64 * half, 64), 64)]

    sent = []

    def push(ref, to, recv):
        copy = pltpu.make_async_remote_copy(
            src_ref=ref, dst_ref=ref, send_sem=w_send.at[len(sent)], recv_sem=recv,
            device_id=to, device_id_type=MESH,
        )
        copy.start()
        sent.append(copy)

    def arrive(ref, sem):
        pltpu.make_async_copy(ref, ref, sem).wait()

    DZ = (0, -1, 1, 2)
    DX = (0, -1, 1, 2)

    def to_x(m, h):
        block = wrows(chip(0, DZ[m]), c, h)
        if h == 0:
            push(block, dev(1, 0), rx.at[m, 0, h])
            push(block, dev(-1, 0), rx.at[m, 1, h])
        else:
            push(block, dev(-1, 0), rx.at[m, 1, h])
            push(block, dev(1, 0), rx.at[m, 0, h])

    def to_sib(m, k):
        push(wrows(chip(DX[k], DZ[m]), c), sib, rsib.at[m, k])

    push(wrows(q, c, 0), dev(0, 1), rz.at[0, 0])
    push(wrows(q, c, 1), dev(0, -1), rz.at[1, 1])
    push(wrows(q, c, 0), dev(1, 0), rx.at[0, 0, 0])
    push(wrows(q, c, 1), dev(-1, 0), rx.at[0, 1, 1])
    push(wrows(q, c, 1), dev(0, 1), rz.at[0, 1])
    push(wrows(q, c, 0), dev(0, -1), rz.at[1, 0])
    push(wrows(q, c, 1), dev(1, 0), rx.at[0, 0, 1])
    push(wrows(q, c, 0), dev(-1, 0), rx.at[0, 1, 0])
    to_sib(0, 0)

    loads[1].wait()
    loads[2].wait()
    ip = dot(acts[...], pin[...], 1, 1)
    for to in range(8):
        block = ip[to * PIECE:(to + 1) * PIECE]
        in_send[to] = jnp.concatenate([block[:128], block[128:]], axis=1).astype(BF16)
    exchange(8, copy_in)
    loads[4].wait()
    copy_panels().start()

    def x_up(m):
        block = wrows(chip(-1, DZ[m]), c, 0)
        arrive(block, rx.at[m, 0, 0])
        push(block, dev(1, 0), rx.at[m, 2, 0])

    def x_down(m):
        block = wrows(chip(1, DZ[m]), c, 1)
        arrive(block, rx.at[m, 1, 1])
        push(block, dev(-1, 0), rx.at[m, 2, 1])

    def x_rest(m):
        arrive(wrows(chip(-1, DZ[m]), c, 1), rx.at[m, 0, 1])
        to_sib(m, 1)
        arrive(wrows(chip(1, DZ[m]), c, 0), rx.at[m, 1, 0])
        to_sib(m, 2)

    def x_far(m):
        arrive(wrows(chip(2, DZ[m]), c, 0), rx.at[m, 2, 0])
        arrive(wrows(chip(2, DZ[m]), c, 1), rx.at[m, 2, 1])
        to_sib(m, 3)

    def z_first():
        arrive(wrows(chip(0, -1), c, 0), rz.at[0, 0])
        push(wrows(chip(0, -1), c, 0), dev(0, 1), rz.at[2, 0])
        to_x(1, 0)
        arrive(wrows(chip(0, 1), c, 1), rz.at[1, 1])
        push(wrows(chip(0, 1), c, 1), dev(0, -1), rz.at[2, 1])
        to_x(2, 1)

    def z_rest():
        arrive(wrows(chip(0, -1), c, 1), rz.at[0, 1])
        to_x(1, 1)
        arrive(wrows(chip(0, 1), c, 0), rz.at[1, 0])
        to_x(2, 0)
        to_sib(1, 0)
        to_sib(2, 0)

    def z_far():
        arrive(wrows(chip(0, 2), c, 0), rz.at[2, 0])
        to_x(3, 0)
        arrive(wrows(chip(0, 2), c, 1), rz.at[2, 1])
        to_x(3, 1)
        to_sib(3, 0)

    for step in range(1, 8):
        cot_load(step).start()

    hear(0)
    tell(1)

    loads[3].wait()
    row = lax.broadcasted_iota(jnp.int32, (64, 64), 0)
    col = lax.broadcasted_iota(jnp.int32, (64, 64), 1)
    even_odd = jnp.where(col == lax.rem(row, 32) * 2 + row // 32, 1.0, 0.0).astype(BF16)
    pout[...] = dot(even_odd, pout[...]).astype(BF16)
    cot_load(0).wait()
    op = dot(cot[pl.ds(pl.multiple_of(j * PIECE, PIECE), PIECE), :], pout[...], 1, 1)
    op_parts = two_parts(jnp.concatenate([op[:128], op[128:]], axis=1))

    def a_pass(first, second, mode):
        for m, k in (first, second):
            arrive(wrows(chip(DX[k], DZ[m]), 1 - c), rsib.at[m, k])
        ka = pl.ds(pl.multiple_of(chip(DX[first[1]], DZ[first[0]]) * 256, 256), 256)
        kb = pl.ds(pl.multiple_of(chip(DX[second[1]], DZ[second[0]]) * 256, 256), 256)
        new = dot(cot[:, ka], wg[ka, :]) + dot(cot[:, kb], wg[kb, :])
        if mode == 0:
            acc[...] = new
        elif mode == 1:
            acc[...] += new
        else:
            act_o[...] = (acc[...] + new).astype(BF16)

    x_up(0)
    x_down(0)
    x_rest(0)
    hear(1)
    tell(2)
    z_first()

    arrive(in_recv.at[pl.ds(0, 7)], e_recv.at[0])
    total = in_send[j].astype(F32)
    for step in range(1, 8):
        total = total + in_recv[lax.rem(j + step, 8)].astype(F32)
    part = dot(op_parts, two_parts(total), 0, 0)
    part = (part[:128, :128] + part[128:, 128:]) + (part[:128, 128:] + part[128:, :128])
    part = part[:64, :64] + part[64:, 64:]
    part = jnp.concatenate([part[:32], part[32:]], axis=1)
    q_part[...] = part
    exchange(8, copy_part)
    q_all[j] = part
    for step in range(1, 8):
        cot_load(step).wait()
    z_rest()
    a_pass((0, 0), (0, 1), 0)
    x_far(0)
    x_up(1)
    x_down(2)
    a_pass((0, 2), (1, 0), 1)

    arrive(q_all.at[pl.ds(0, 7)], e_recv.at[1])
    for e in range(4):
        grads = (q_all[2 * e] + q_all[2 * e + 1]) * (1.0 / math.sqrt(LEN))
        for t in range(8):
            tiles_f[t, e * 4:e * 4 + 4, :] = grads[t * 4:t * 4 + 4]
    tiles[...] = tiles_f[...].astype(BF16)
    hear(2)
    exchange(16, copy_grads)
    exchange(16, copy_cols)
    g_rows_all[c, q] = tiles[q // 2]
    g_cols_all[c, q] = tiles[j]
    z_far()
    x_down(1)
    x_up(2)
    a_pass((2, 0), (0, 3), 1)
    x_rest(1)
    x_rest(2)
    a_pass((3, 0), (1, 1), 1)

    m = lax.broadcasted_iota(jnp.int32, (64, 256), 0)
    n = lax.broadcasted_iota(jnp.int32, (64, 256), 1)
    pick = [jnp.where(n == m * 4 + lax.rem(q, 2) * 2 + u, 1.0, 0.0).astype(BF16) for u in range(2)]
    arrive(pan.at[1 - c], e_recv.at[5])
    arrive(g_rows_all.at[c, pl.ds(0, 15)], e_recv.at[2])
    own_tiles = g_rows_all[c].reshape(256, 128)
    score = dot(dot(pick[0], own_tiles).astype(BF16), pan[0])
    score += dot(dot(pick[1], own_tiles).astype(BF16), pan[1])
    for to in range(16):
        s_part[to] = score[to * 4:to * 4 + 4]
    exchange(16, copy_scores)
    x_up(3)
    x_down(3)
    copy_pair().start()
    arrive(g_cols_all.at[c, pl.ds(0, 15)], e_recv.at[6])
    copy_pair_cols().start()
    x_far(1)
    x_far(2)
    a_pass((1, 2), (2, 1), 1)
    x_rest(3)
    a_pass((2, 2), (1, 3), 1)
    x_far(3)
    a_pass((2, 3), (3, 1), 1)

    arrive(g_rows_all.at[1 - c], e_recv.at[3])
    arrive(g_cols_all.at[1 - c], e_recv.at[7])
    m = lax.broadcasted_iota(jnp.int32, (128, 512), 0)
    n = lax.broadcasted_iota(jnp.int32, (128, 512), 1)

    def select(r):
        return jnp.where(n == m * 4 + r, 1.0, 0.0).astype(BF16)

    row_tiles = g_rows_all[...].reshape(512, 128)
    col_tiles = g_cols_all[...].reshape(512, 128)
    g_rows = dot(select(lax.rem(i, 4)), row_tiles).astype(BF16)
    g_cols = jnp.concatenate([dot(select(r), col_tiles).astype(BF16) for r in range(4)], axis=1)
    fish_o[...] = dot(g_rows, g_cols, 0, 0) * (1.0 / 128)
    a_pass((3, 2), (3, 3), 2)

    arrive(s_recv.at[pl.ds(0, 15)], e_recv.at[4])
    total = s_part[q]
    for step in range(1, 16):
        total = total + s_recv[lax.rem(q + step, 16)]
    score_o[...] = total

    for copy in sent:
        copy.wait_send()
    done_sending(8, copy_in)
    done_sending(8, copy_part)
    done_sending(16, copy_grads)
    done_sending(16, copy_cols)
    copy_pair_cols().wait_send()
    done_sending(16, copy_scores)
    copy_pair().wait_send()
    copy_panels().wait_send()


def write_out(act, fish, score, act_o, fish_o, score_o, sem):
    copies = [
        pltpu.make_async_copy(src, dst, sem.at[n])
        for n, (src, dst) in enumerate(((act, act_o), (fish, fish_o), (score, score_o)))
    ]
    for copy in copies:
        copy.start()
    for copy in copies:
        copy.wait()


def per_device(acts, cotangent, out_weight, proj_in, proj_out, panels):
    rows, wide = cotangent.shape
    feats = acts.shape[1]
    any_spec = pl.BlockSpec(memory_space=pl.ANY)
    vmem_spec = pl.BlockSpec(memory_space=pltpu.VMEM)
    dma = pltpu.SemaphoreType.DMA
    operands = (acts, cotangent, out_weight, proj_in.T, proj_out.T, panels)
    operands = [pltpu.with_memory_space_constraint(a, pltpu.HBM) for a in operands]
    results = (
        ((rows, feats), BF16),
        ((128, 512), F32),
        ((4, 512), F32),
    )
    held = pl.pallas_call(
        kernel,
        out_shape=tuple(pltpu.VMEM(*r) for r in results),
        in_specs=[any_spec] * 6,
        out_specs=(vmem_spec, vmem_spec, vmem_spec),
        scratch_shapes=[
            pltpu.VMEM((rows, feats), BF16),
            pltpu.VMEM((rows, wide), BF16),
            pltpu.VMEM((feats, 128), BF16),
            pltpu.VMEM((64, feats), BF16),
            pltpu.VMEM((64, wide), BF16),
            pltpu.VMEM((2, 128, 512), BF16),
            pltpu.VMEM((wide, feats), BF16),
            pltpu.VMEM((rows, feats), F32),
            pltpu.VMEM((8, 128, 128), BF16),
            pltpu.VMEM((8, 128, 128), BF16),
            pltpu.VMEM((32, 128), F32),
            pltpu.VMEM((8, 32, 128), F32),
            pltpu.VMEM((8, 16, 128), F32),
            pltpu.VMEM((8, 16, 128), BF16),
            pltpu.VMEM((2, 16, 16, 128), BF16),
            pltpu.VMEM((2, 16, 16, 128), BF16),
            pltpu.VMEM((16, 4, 512), F32),
            pltpu.VMEM((16, 4, 512), F32),
            dma((5,)),
            dma((8,)),
            dma((46,)),
            dma((3, 2)),
            dma((4, 3, 2)),
            dma((4, 4)),
            dma((8, 16)),
            dma((8,)),
            pltpu.SemaphoreType.REGULAR((3,)),
        ],
        compiler_params=pltpu.CompilerParams(
            collective_id=0, has_side_effects=True, vmem_limit_bytes=40 * 1024 * 1024
        ),
        cost_estimate=pl.CostEstimate(
            flops=2 * rows * wide * (feats + 64), bytes_accessed=26 * 2**20, transcendentals=0
        ),
    )(*operands)
    return pl.pallas_call(
        write_out,
        out_shape=tuple(jax.ShapeDtypeStruct(*r) for r in results),
        in_specs=[vmem_spec] * 3,
        out_specs=(any_spec,) * 3,
        scratch_shapes=[dma((3,))],
    )(*(pltpu.with_memory_space_constraint(h, pltpu.VMEM) for h in held))


def solution(mesh):
    return jax.shard_map(
        per_device,
        mesh=mesh,
        in_specs=(
            P("dp", "fisher"),
            P("dp", None),
            P("fisher", "dp"),
            P("fisher", None),
            P(),
            P("dp", "fisher"),
        ),
        out_specs=(P("dp", "fisher"), P("dp", "fisher"), P("dp", "fisher")),
        check_vma=False,
    )
```

```python
import functools
import math

import jax
import jax.numpy as jnp
from jax import lax
from jax.experimental import pallas as pl
from jax.experimental.pallas import tpu as pltpu
from jax.sharding import PartitionSpec as P

LEN = 512
MESH = pl.DeviceIdType.MESH
F32 = jnp.float32
BF16 = jnp.bfloat16
PIECE = 256


def dot(a, b, ca=1, cb=0, precision=None):
    return lax.dot_general(
        a, b, (((ca,), (cb,)), ((), ())), preferred_element_type=F32, precision=precision
    )


def two_parts(v):
    high = v.astype(BF16)
    return jnp.concatenate([high, (v - high.astype(F32)).astype(BF16)], axis=1)


def kernel(
    acts_h, cot_h, w_h, pin_h, pout_h, pan_h,
    act_o, fish_o, score_o,
    acts, cot, w_own, pin, pout, pan, wg, acc,
    in_send, in_recv, q_part, q_all, tiles_f, tiles, g_rows_all, g_cols_all, s_part, s_recv,
    in_sem, cot_sem,
    w_send, rz, rx, rsib,
    e_send, e_recv, word,
):
    i = lax.axis_index("dp")
    j = lax.axis_index("fisher")
    c = lax.rem(i, 2)
    q = i // 2
    zh = lax.rem(q, 4)
    x = q // 4
    sib = (i + 1 - 2 * c, j)

    def chip(dx, dz):
        return lax.rem(x + dx + 4, 4) * 4 + lax.rem(zh + dz + 4, 4)

    def dev(dx, dz):
        return (chip(dx, dz) * 2 + c, j)

    loads = [
        pltpu.make_async_copy(w_h, w_own, in_sem.at[0]),
        pltpu.make_async_copy(acts_h, acts, in_sem.at[1]),
        pltpu.make_async_copy(pin_h, pin, in_sem.at[2]),
        pltpu.make_async_copy(pout_h, pout, in_sem.at[3]),
        pltpu.make_async_copy(pan_h, pan.at[c], in_sem.at[4]),
    ]

    def cot_load(s):
        rows = pl.ds(pl.multiple_of(lax.rem(j + s, 8) * PIECE, PIECE), PIECE)
        return pltpu.make_async_copy(cot_h.at[rows], cot.at[rows], cot_sem.at[s])

    for load in loads[:3]:
        load.start()

    barrier = pltpu.get_barrier_semaphore()
    pl.semaphore_signal(barrier, inc=1, device_id=sib, device_id_type=MESH)

    @pl.loop(1, 8)
    def _(s):
        pl.semaphore_signal(barrier, inc=1, device_id=(i, lax.rem(j + s, 8)), device_id_type=MESH)

    for near in (dev(1, 0), dev(-1, 0), dev(0, 1), dev(0, -1)):
        pl.semaphore_signal(barrier, inc=1, device_id=near, device_id_type=MESH)

    for load in loads[3:]:
        load.start()
    cot_load(0).start()

    eye = jnp.where(
        lax.broadcasted_iota(jnp.int32, (128, 128), 0) == lax.broadcasted_iota(jnp.int32, (128, 128), 1),
        1.0, 0.0,
    ).astype(BF16)
    loads[0].wait()
    wg[pl.ds(pl.multiple_of(q * 256 + c * 128, 128), 128), :] = dot(eye, w_own[...], 1, 1).astype(BF16)

    pl.semaphore_wait(barrier, 12)

    def tell(k):
        for to in ((dev(1, 0), dev(-1, 0)) if k == 0 else (dev(0, 1), dev(0, -1))):
            pl.semaphore_signal(word.at[k], inc=1, device_id=to, device_id_type=MESH)

    def hear(k):
        pl.semaphore_wait(word.at[k], 2)

    tell(0)

    def remote(src, dst, to, stage, s=0):
        return pltpu.make_async_remote_copy(
            src_ref=src, dst_ref=dst, send_sem=e_send.at[stage, s], recv_sem=e_recv.at[stage],
            device_id=to, device_id_type=MESH,
        )

    def copy_in(s):
        to = lax.rem(j + s, 8)
        return remote(in_send.at[to], in_recv.at[j], (i, to), 0, s)

    def copy_part(s):
        return remote(q_part, q_all.at[j], (i, lax.rem(j + s, 8)), 1, s)

    def copy_grads(s):
        to = lax.rem(q + s, 16)
        return remote(tiles.at[to // 2], g_rows_all.at[c, q], (to * 2 + c, j), 2, s)

    def copy_cols(s):
        to = lax.rem(q + s, 16)
        return remote(tiles.at[j], g_cols_all.at[c, q], (to * 2 + c, j), 6, s)

    def copy_pair():
        return remote(g_rows_all.at[c], g_rows_all.at[c], sib, 3)

    def copy_pair_cols():
        return remote(g_cols_all.at[c], g_cols_all.at[c], sib, 7)

    def copy_scores(s):
        to = lax.rem(q + s, 16)
        return remote(s_part.at[to], s_recv.at[q], (to * 2 + c, j), 4, s)

    def copy_panels():
        return remote(pan.at[c], pan.at[c], sib, 5)

    def exchange(n, copy_of):
        def go(s, _):
            copy_of(s).start()
            return 0
        lax.fori_loop(1, n, go, 0)

    def done_sending(n, copy_of):
        def go(s, _):
            copy_of(s).wait_send()
            return 0
        lax.fori_loop(1, n, go, 0)

    def wrows(chip_index, core, half=None):
        start = chip_index * 256 + core * 128
        if half is None:
            return wg.at[pl.ds(pl.multiple_of(start, 128), 128)]
        return wg.at[pl.ds(pl.multiple_of(start + 64 * half, 64), 64)]

    sent = []

    def push(ref, to, recv):
        copy = pltpu.make_async_remote_copy(
            src_ref=ref, dst_ref=ref, send_sem=w_send.at[len(sent)], recv_sem=recv,
            device_id=to, device_id_type=MESH,
        )
        copy.start()
        sent.append(copy)

    def arrive(ref, sem):
        pltpu.make_async_copy(ref, ref, sem).wait()

    DZ = (0, -1, 1, 2)
    DX = (0, -1, 1, 2)

    def to_x(m, h):
        block = wrows(chip(0, DZ[m]), c, h)
        if h == 0:
            push(block, dev(1, 0), rx.at[m, 0, h])
            push(block, dev(-1, 0), rx.at[m, 1, h])
        else:
            push(block, dev(-1, 0), rx.at[m, 1, h])
            push(block, dev(1, 0), rx.at[m, 0, h])

    def to_sib(m, k):
        push(wrows(chip(DX[k], DZ[m]), c), sib, rsib.at[m, k])

    push(wrows(q, c, 0), dev(0, 1), rz.at[0, 0])
    push(wrows(q, c, 1), dev(0, -1), rz.at[1, 1])
    push(wrows(q, c, 1), dev(0, 1), rz.at[0, 1])
    push(wrows(q, c, 0), dev(0, -1), rz.at[1, 0])
    push(wrows(q, c, 0), dev(1, 0), rx.at[0, 0, 0])
    push(wrows(q, c, 1), dev(-1, 0), rx.at[0, 1, 1])
    push(wrows(q, c, 1), dev(1, 0), rx.at[0, 0, 1])
    push(wrows(q, c, 0), dev(-1, 0), rx.at[0, 1, 0])
    to_sib(0, 0)

    loads[1].wait()
    loads[2].wait()
    ip = dot(acts[...], pin[...], 1, 1)
    for to in range(8):
        block = ip[to * PIECE:(to + 1) * PIECE]
        in_send[to] = jnp.concatenate([block[:128], block[128:]], axis=1).astype(BF16)
    exchange(8, copy_in)
    loads[4].wait()
    copy_panels().start()

    def x_up(m):
        block = wrows(chip(-1, DZ[m]), c, 0)
        arrive(block, rx.at[m, 0, 0])
        push(block, dev(1, 0), rx.at[m, 2, 0])

    def x_down(m):
        block = wrows(chip(1, DZ[m]), c, 1)
        arrive(block, rx.at[m, 1, 1])
        push(block, dev(-1, 0), rx.at[m, 2, 1])

    def x_rest(m):
        arrive(wrows(chip(-1, DZ[m]), c, 1), rx.at[m, 0, 1])
        to_sib(m, 1)
        arrive(wrows(chip(1, DZ[m]), c, 0), rx.at[m, 1, 0])
        to_sib(m, 2)

    def x_far(m):
        arrive(wrows(chip(2, DZ[m]), c, 0), rx.at[m, 2, 0])
        arrive(wrows(chip(2, DZ[m]), c, 1), rx.at[m, 2, 1])
        to_sib(m, 3)

    def z_first():
        arrive(wrows(chip(0, -1), c, 0), rz.at[0, 0])
        push(wrows(chip(0, -1), c, 0), dev(0, 1), rz.at[2, 0])
        to_x(1, 0)
        arrive(wrows(chip(0, 1), c, 1), rz.at[1, 1])
        push(wrows(chip(0, 1), c, 1), dev(0, -1), rz.at[2, 1])
        to_x(2, 1)

    def z_rest():
        arrive(wrows(chip(0, -1), c, 1), rz.at[0, 1])
        to_x(1, 1)
        arrive(wrows(chip(0, 1), c, 0), rz.at[1, 0])
        to_x(2, 0)
        to_sib(1, 0)
        to_sib(2, 0)

    def z_far():
        arrive(wrows(chip(0, 2), c, 0), rz.at[2, 0])
        to_x(3, 0)
        arrive(wrows(chip(0, 2), c, 1), rz.at[2, 1])
        to_x(3, 1)
        to_sib(3, 0)

    for step in range(1, 8):
        cot_load(step).start()

    hear(0)
    tell(1)

    loads[3].wait()
    row = lax.broadcasted_iota(jnp.int32, (64, 64), 0)
    col = lax.broadcasted_iota(jnp.int32, (64, 64), 1)
    even_odd = jnp.where(col == lax.rem(row, 32) * 2 + row // 32, 1.0, 0.0).astype(BF16)
    pout[...] = dot(even_odd, pout[...]).astype(BF16)
    cot_load(0).wait()
    op = dot(cot[pl.ds(pl.multiple_of(j * PIECE, PIECE), PIECE), :], pout[...], 1, 1)
    op_parts = two_parts(jnp.concatenate([op[:128], op[128:]], axis=1))

    def a_pass(first, second, mode):
        for m, k in (first, second):
            arrive(wrows(chip(DX[k], DZ[m]), 1 - c), rsib.at[m, k])
        ka = pl.ds(pl.multiple_of(chip(DX[first[1]], DZ[first[0]]) * 256, 256), 256)
        kb = pl.ds(pl.multiple_of(chip(DX[second[1]], DZ[second[0]]) * 256, 256), 256)
        new = dot(cot[:, ka], wg[ka, :]) + dot(cot[:, kb], wg[kb, :])
        if mode == 0:
            acc[...] = new
        elif mode == 1:
            acc[...] += new
        else:
            act_o[...] = (acc[...] + new).astype(BF16)

    x_up(0)
    x_down(0)
    x_rest(0)
    hear(1)
    tell(2)
    z_first()

    arrive(in_recv.at[pl.ds(0, 7)], e_recv.at[0])
    total = in_send[j].astype(F32)
    for step in range(1, 8):
        total = total + in_recv[lax.rem(j + step, 8)].astype(F32)
    part = dot(op_parts, two_parts(total), 0, 0)
    part = (part[:128, :128] + part[128:, 128:]) + (part[:128, 128:] + part[128:, :128])
    part = part[:64, :64] + part[64:, 64:]
    part = jnp.concatenate([part[:32], part[32:]], axis=1)
    q_part[...] = part
    exchange(8, copy_part)
    q_all[j] = part
    for step in range(1, 8):
        cot_load(step).wait()
    z_rest()
    a_pass((0, 0), (0, 1), 0)
    x_far(0)
    x_up(1)
    x_down(2)
    a_pass((0, 2), (1, 0), 1)

    arrive(q_all.at[pl.ds(0, 7)], e_recv.at[1])
    for e in range(4):
        grads = (q_all[2 * e] + q_all[2 * e + 1]) * (1.0 / math.sqrt(LEN))
        for t in range(8):
            tiles_f[t, e * 4:e * 4 + 4, :] = grads[t * 4:t * 4 + 4]
    tiles[...] = tiles_f[...].astype(BF16)
    hear(2)
    exchange(16, copy_grads)
    exchange(16, copy_cols)
    g_rows_all[c, q] = tiles[q // 2]
    g_cols_all[c, q] = tiles[j]
    z_far()
    x_down(1)
    x_up(2)
    x_rest(1)
    x_rest(2)
    a_pass((2, 0), (0, 3), 1)
    x_up(3)
    x_down(3)
    a_pass((3, 0), (1, 1), 1)

    m = lax.broadcasted_iota(jnp.int32, (64, 256), 0)
    n = lax.broadcasted_iota(jnp.int32, (64, 256), 1)
    pick = [jnp.where(n == m * 4 + lax.rem(q, 2) * 2 + u, 1.0, 0.0).astype(BF16) for u in range(2)]
    arrive(pan.at[1 - c], e_recv.at[5])
    arrive(g_rows_all.at[c, pl.ds(0, 15)], e_recv.at[2])
    own_tiles = g_rows_all[c].reshape(256, 128)
    score = dot(dot(pick[0], own_tiles).astype(BF16), pan[0])
    score += dot(dot(pick[1], own_tiles).astype(BF16), pan[1])
    for to in range(16):
        s_part[to] = score[to * 4:to * 4 + 4]
    exchange(16, copy_scores)
    copy_pair().start()
    arrive(g_cols_all.at[c, pl.ds(0, 15)], e_recv.at[6])
    copy_pair_cols().start()
    x_far(1)
    x_far(2)
    a_pass((1, 2), (2, 1), 1)
    x_rest(3)
    a_pass((2, 2), (1, 3), 1)
    arrive(g_rows_all.at[1 - c], e_recv.at[3])
    arrive(g_cols_all.at[1 - c], e_recv.at[7])
    m = lax.broadcasted_iota(jnp.int32, (128, 512), 0)
    n = lax.broadcasted_iota(jnp.int32, (128, 512), 1)

    def select(r):
        return jnp.where(n == m * 4 + r, 1.0, 0.0).astype(BF16)

    row_tiles = g_rows_all[...].reshape(512, 128)
    col_tiles = g_cols_all[...].reshape(512, 128)
    g_rows = dot(select(lax.rem(i, 4)), row_tiles).astype(BF16)
    g_cols = jnp.concatenate([dot(select(r), col_tiles).astype(BF16) for r in range(4)], axis=1)
    fish_o[...] = dot(g_rows, g_cols, 0, 0) * (1.0 / 128)

    x_far(3)
    a_pass((2, 3), (3, 1), 1)

    a_pass((3, 2), (3, 3), 2)

    arrive(s_recv.at[pl.ds(0, 15)], e_recv.at[4])
    total = s_part[q]
    for step in range(1, 16):
        total = total + s_recv[lax.rem(q + step, 16)]
    score_o[...] = total

    for copy in sent:
        copy.wait_send()
    done_sending(8, copy_in)
    done_sending(8, copy_part)
    done_sending(16, copy_grads)
    done_sending(16, copy_cols)
    copy_pair_cols().wait_send()
    done_sending(16, copy_scores)
    copy_pair().wait_send()
    copy_panels().wait_send()


def write_out(act, fish, score, act_o, fish_o, score_o, sem):
    copies = [
        pltpu.make_async_copy(src, dst, sem.at[n])
        for n, (src, dst) in enumerate(((act, act_o), (fish, fish_o), (score, score_o)))
    ]
    for copy in copies:
        copy.start()
    for copy in copies:
        copy.wait()


def per_device(acts, cotangent, out_weight, proj_in, proj_out, panels):
    rows, wide = cotangent.shape
    feats = acts.shape[1]
    any_spec = pl.BlockSpec(memory_space=pl.ANY)
    vmem_spec = pl.BlockSpec(memory_space=pltpu.VMEM)
    dma = pltpu.SemaphoreType.DMA
    operands = (acts, cotangent, out_weight, proj_in.T, proj_out.T, panels)
    operands = [pltpu.with_memory_space_constraint(a, pltpu.HBM) for a in operands]
    results = (
        ((rows, feats), BF16),
        ((128, 512), F32),
        ((4, 512), F32),
    )
    held = pl.pallas_call(
        kernel,
        out_shape=tuple(pltpu.VMEM(*r) for r in results),
        in_specs=[any_spec] * 6,
        out_specs=(vmem_spec, vmem_spec, vmem_spec),
        scratch_shapes=[
            pltpu.VMEM((rows, feats), BF16),
            pltpu.VMEM((rows, wide), BF16),
            pltpu.VMEM((feats, 128), BF16),
            pltpu.VMEM((64, feats), BF16),
            pltpu.VMEM((64, wide), BF16),
            pltpu.VMEM((2, 128, 512), BF16),
            pltpu.VMEM((wide, feats), BF16),
            pltpu.VMEM((rows, feats), F32),
            pltpu.VMEM((8, 128, 128), BF16),
            pltpu.VMEM((8, 128, 128), BF16),
            pltpu.VMEM((32, 128), F32),
            pltpu.VMEM((8, 32, 128), F32),
            pltpu.VMEM((8, 16, 128), F32),
            pltpu.VMEM((8, 16, 128), BF16),
            pltpu.VMEM((2, 16, 16, 128), BF16),
            pltpu.VMEM((2, 16, 16, 128), BF16),
            pltpu.VMEM((16, 4, 512), F32),
            pltpu.VMEM((16, 4, 512), F32),
            dma((5,)),
            dma((8,)),
            dma((46,)),
            dma((3, 2)),
            dma((4, 3, 2)),
            dma((4, 4)),
            dma((8, 16)),
            dma((8,)),
            pltpu.SemaphoreType.REGULAR((3,)),
        ],
        compiler_params=pltpu.CompilerParams(
            collective_id=0, has_side_effects=True, vmem_limit_bytes=40 * 1024 * 1024
        ),
        cost_estimate=pl.CostEstimate(
            flops=2 * rows * wide * (feats + 64), bytes_accessed=26 * 2**20, transcendentals=0
        ),
    )(*operands)
    return pl.pallas_call(
        write_out,
        out_shape=tuple(jax.ShapeDtypeStruct(*r) for r in results),
        in_specs=[vmem_spec] * 3,
        out_specs=(any_spec,) * 3,
        scratch_shapes=[dma((3,))],
    )(*(pltpu.with_memory_space_constraint(h, pltpu.VMEM) for h in held))


def solution(mesh):
    return jax.shard_map(
        per_device,
        mesh=mesh,
        in_specs=(
            P("dp", "fisher"),
            P("dp", None),
            P("fisher", "dp"),
            P("fisher", None),
            P(),
            P("dp", "fisher"),
        ),
        out_specs=(P("dp", "fisher"), P("dp", "fisher"), P("dp", "fisher")),
        check_vma=False,
    )
```

```python
import functools
import math

import jax
import jax.numpy as jnp
from jax import lax
from jax.experimental import pallas as pl
from jax.experimental.pallas import tpu as pltpu
from jax.sharding import PartitionSpec as P

LEN = 512
MESH = pl.DeviceIdType.MESH
F32 = jnp.float32
BF16 = jnp.bfloat16
PIECE = 256


def dot(a, b, ca=1, cb=0, precision=None):
    return lax.dot_general(
        a, b, (((ca,), (cb,)), ((), ())), preferred_element_type=F32, precision=precision
    )


def two_parts(v):
    high = v.astype(BF16)
    return jnp.concatenate([high, (v - high.astype(F32)).astype(BF16)], axis=1)


def kernel(
    acts_h, cot_h, w_h, pin_h, pout_h, pan_h,
    act_o, fish_o, score_o,
    acts, cot, w_own, pin, pout, pan, wg, acc,
    in_send, in_recv, q_part, q_all, tiles_f, tiles, g_rows_all, g_cols_all, s_part, s_recv,
    in_sem, cot_sem,
    w_send, rz, rx, rsib,
    e_send, e_recv, word,
):
    i = lax.axis_index("dp")
    j = lax.axis_index("fisher")
    c = lax.rem(i, 2)
    q = i // 2
    zh = lax.rem(q, 4)
    x = q // 4
    sib = (i + 1 - 2 * c, j)

    def chip(dx, dz):
        return lax.rem(x + dx + 4, 4) * 4 + lax.rem(zh + dz + 4, 4)

    def dev(dx, dz):
        return (chip(dx, dz) * 2 + c, j)

    loads = [
        pltpu.make_async_copy(w_h, w_own, in_sem.at[0]),
        pltpu.make_async_copy(acts_h, acts, in_sem.at[1]),
        pltpu.make_async_copy(pin_h, pin, in_sem.at[2]),
        pltpu.make_async_copy(pout_h, pout, in_sem.at[3]),
        pltpu.make_async_copy(pan_h, pan.at[c], in_sem.at[4]),
    ]

    def cot_load(s):
        rows = pl.ds(pl.multiple_of(lax.rem(j + s, 8) * PIECE, PIECE), PIECE)
        return pltpu.make_async_copy(cot_h.at[rows], cot.at[rows], cot_sem.at[s])

    for load in loads[:3]:
        load.start()

    barrier = pltpu.get_barrier_semaphore()
    pl.semaphore_signal(barrier, inc=1, device_id=sib, device_id_type=MESH)

    @pl.loop(1, 8)
    def _(s):
        pl.semaphore_signal(barrier, inc=1, device_id=(i, lax.rem(j + s, 8)), device_id_type=MESH)

    for near in (dev(1, 0), dev(-1, 0), dev(0, 1), dev(0, -1)):
        pl.semaphore_signal(barrier, inc=1, device_id=near, device_id_type=MESH)

    for load in loads[3:]:
        load.start()
    cot_load(0).start()

    eye = jnp.where(
        lax.broadcasted_iota(jnp.int32, (128, 128), 0) == lax.broadcasted_iota(jnp.int32, (128, 128), 1),
        1.0, 0.0,
    ).astype(BF16)
    loads[0].wait()
    wg[pl.ds(pl.multiple_of(q * 256 + c * 128, 128), 128), :] = dot(eye, w_own[...], 1, 1).astype(BF16)

    pl.semaphore_wait(barrier, 12)

    def tell(k):
        for to in ((dev(1, 0), dev(-1, 0)) if k == 0 else (dev(0, 1), dev(0, -1))):
            pl.semaphore_signal(word.at[k], inc=1, device_id=to, device_id_type=MESH)

    def hear(k):
        pl.semaphore_wait(word.at[k], 2)

    tell(0)

    def remote(src, dst, to, stage, s=0):
        return pltpu.make_async_remote_copy(
            src_ref=src, dst_ref=dst, send_sem=e_send.at[stage, s], recv_sem=e_recv.at[stage],
            device_id=to, device_id_type=MESH,
        )

    def copy_in(s):
        to = lax.rem(j + s, 8)
        return remote(in_send.at[to], in_recv.at[j], (i, to), 0, s)

    def copy_part(s):
        return remote(q_part, q_all.at[j], (i, lax.rem(j + s, 8)), 1, s)

    def copy_grads(s):
        to = lax.rem(q + s, 16)
        return remote(tiles.at[to // 2], g_rows_all.at[c, q], (to * 2 + c, j), 2, s)

    def copy_cols(s):
        to = lax.rem(q + s, 16)
        return remote(tiles.at[j], g_cols_all.at[c, q], (to * 2 + c, j), 6, s)

    def copy_pair():
        return remote(g_rows_all.at[c], g_rows_all.at[c], sib, 3)

    def copy_pair_cols():
        return remote(g_cols_all.at[c], g_cols_all.at[c], sib, 7)

    def copy_scores(s):
        to = lax.rem(q + s, 16)
        return remote(s_part.at[to], s_recv.at[q], (to * 2 + c, j), 4, s)

    def copy_panels():
        return remote(pan.at[c], pan.at[c], sib, 5)

    def exchange(n, copy_of):
        def go(s, _):
            copy_of(s).start()
            return 0
        lax.fori_loop(1, n, go, 0)

    def done_sending(n, copy_of):
        def go(s, _):
            copy_of(s).wait_send()
            return 0
        lax.fori_loop(1, n, go, 0)

    def wrows(chip_index, core, half=None):
        start = chip_index * 256 + core * 128
        if half is None:
            return wg.at[pl.ds(pl.multiple_of(start, 128), 128)]
        return wg.at[pl.ds(pl.multiple_of(start + 64 * half, 64), 64)]

    sent = []

    def push(ref, to, recv):
        copy = pltpu.make_async_remote_copy(
            src_ref=ref, dst_ref=ref, send_sem=w_send.at[len(sent)], recv_sem=recv,
            device_id=to, device_id_type=MESH,
        )
        copy.start()
        sent.append(copy)

    def arrive(ref, sem):
        pltpu.make_async_copy(ref, ref, sem).wait()

    DZ = (0, -1, 1, 2)
    DX = (0, -1, 1, 2)

    def to_x(m, h):
        block = wrows(chip(0, DZ[m]), c, h)
        if h == 0:
            push(block, dev(1, 0), rx.at[m, 0, h])
            push(block, dev(-1, 0), rx.at[m, 1, h])
        else:
            push(block, dev(-1, 0), rx.at[m, 1, h])
            push(block, dev(1, 0), rx.at[m, 0, h])

    def to_sib(m, k):
        push(wrows(chip(DX[k], DZ[m]), c), sib, rsib.at[m, k])

    push(wrows(q, c, 0), dev(0, 1), rz.at[0, 0])
    push(wrows(q, c, 1), dev(0, -1), rz.at[1, 1])
    push(wrows(q, c, 1), dev(0, 1), rz.at[0, 1])
    push(wrows(q, c, 0), dev(0, -1), rz.at[1, 0])
    push(wrows(q, c, 0), dev(1, 0), rx.at[0, 0, 0])
    push(wrows(q, c, 1), dev(-1, 0), rx.at[0, 1, 1])
    push(wrows(q, c, 1), dev(1, 0), rx.at[0, 0, 1])
    push(wrows(q, c, 0), dev(-1, 0), rx.at[0, 1, 0])
    to_sib(0, 0)

    loads[1].wait()
    loads[2].wait()
    ip = dot(acts[...], pin[...], 1, 1)
    for to in range(8):
        block = ip[to * PIECE:(to + 1) * PIECE]
        in_send[to] = jnp.concatenate([block[:128], block[128:]], axis=1).astype(BF16)
    exchange(8, copy_in)
    loads[4].wait()
    copy_panels().start()

    def x_up(m):
        block = wrows(chip(-1, DZ[m]), c, 0)
        arrive(block, rx.at[m, 0, 0])
        push(block, dev(1, 0), rx.at[m, 2, 0])

    def x_down(m):
        block = wrows(chip(1, DZ[m]), c, 1)
        arrive(block, rx.at[m, 1, 1])
        push(block, dev(-1, 0), rx.at[m, 2, 1])

    def x_rest(m):
        arrive(wrows(chip(-1, DZ[m]), c, 1), rx.at[m, 0, 1])
        to_sib(m, 1)
        arrive(wrows(chip(1, DZ[m]), c, 0), rx.at[m, 1, 0])
        to_sib(m, 2)

    def x_far(m):
        arrive(wrows(chip(2, DZ[m]), c, 0), rx.at[m, 2, 0])
        arrive(wrows(chip(2, DZ[m]), c, 1), rx.at[m, 2, 1])
        to_sib(m, 3)

    def z_first():
        arrive(wrows(chip(0, -1), c, 0), rz.at[0, 0])
        push(wrows(chip(0, -1), c, 0), dev(0, 1), rz.at[2, 0])
        to_x(1, 0)
        arrive(wrows(chip(0, 1), c, 1), rz.at[1, 1])
        push(wrows(chip(0, 1), c, 1), dev(0, -1), rz.at[2, 1])
        to_x(2, 1)

    def z_rest():
        arrive(wrows(chip(0, -1), c, 1), rz.at[0, 1])
        to_x(1, 1)
        arrive(wrows(chip(0, 1), c, 0), rz.at[1, 0])
        to_x(2, 0)
        to_sib(1, 0)
        to_sib(2, 0)

    def z_far():
        arrive(wrows(chip(0, 2), c, 0), rz.at[2, 0])
        to_x(3, 0)
        arrive(wrows(chip(0, 2), c, 1), rz.at[2, 1])
        to_x(3, 1)
        to_sib(3, 0)

    for step in range(1, 8):
        cot_load(step).start()

    hear(0)
    tell(1)

    loads[3].wait()
    row = lax.broadcasted_iota(jnp.int32, (64, 64), 0)
    col = lax.broadcasted_iota(jnp.int32, (64, 64), 1)
    even_odd = jnp.where(col == lax.rem(row, 32) * 2 + row // 32, 1.0, 0.0).astype(BF16)
    pout[...] = dot(even_odd, pout[...]).astype(BF16)
    cot_load(0).wait()
    op = dot(cot[pl.ds(pl.multiple_of(j * PIECE, PIECE), PIECE), :], pout[...], 1, 1)
    op_parts = two_parts(jnp.concatenate([op[:128], op[128:]], axis=1))

    def a_pass(first, second, mode):
        for m, k in (first, second):
            arrive(wrows(chip(DX[k], DZ[m]), 1 - c), rsib.at[m, k])
        ka = pl.ds(pl.multiple_of(chip(DX[first[1]], DZ[first[0]]) * 256, 256), 256)
        kb = pl.ds(pl.multiple_of(chip(DX[second[1]], DZ[second[0]]) * 256, 256), 256)
        new = dot(cot[:, ka], wg[ka, :]) + dot(cot[:, kb], wg[kb, :])
        if mode == 0:
            acc[...] = new
        elif mode == 1:
            acc[...] += new
        else:
            act_o[...] = (acc[...] + new).astype(BF16)

    x_up(0)
    x_down(0)
    x_rest(0)
    hear(1)
    tell(2)
    z_first()

    arrive(in_recv.at[pl.ds(0, 7)], e_recv.at[0])
    total = in_send[j].astype(F32)
    for step in range(1, 8):
        total = total + in_recv[lax.rem(j + step, 8)].astype(F32)
    part = dot(op_parts, two_parts(total), 0, 0)
    part = (part[:128, :128] + part[128:, 128:]) + (part[:128, 128:] + part[128:, :128])
    part = part[:64, :64] + part[64:, 64:]
    part = jnp.concatenate([part[:32], part[32:]], axis=1)
    q_part[...] = part
    exchange(8, copy_part)
    q_all[j] = part
    for step in range(1, 8):
        cot_load(step).wait()
    z_rest()
    a_pass((0, 0), (0, 1), 0)
    x_far(0)
    x_up(1)
    x_down(2)
    a_pass((0, 2), (1, 0), 1)

    arrive(q_all.at[pl.ds(0, 7)], e_recv.at[1])
    for e in range(4):
        grads = (q_all[2 * e] + q_all[2 * e + 1]) * (1.0 / math.sqrt(LEN))
        for t in range(8):
            tiles_f[t, e * 4:e * 4 + 4, :] = grads[t * 4:t * 4 + 4]
    tiles[...] = tiles_f[...].astype(BF16)
    hear(2)
    exchange(16, copy_grads)
    exchange(16, copy_cols)
    g_rows_all[c, q] = tiles[q // 2]
    g_cols_all[c, q] = tiles[j]
    z_far()
    x_down(1)
    x_up(2)
    x_rest(1)
    x_rest(2)
    a_pass((2, 0), (0, 3), 1)
    x_up(3)
    x_down(3)
    a_pass((3, 0), (1, 1), 1)

    m = lax.broadcasted_iota(jnp.int32, (64, 256), 0)
    n = lax.broadcasted_iota(jnp.int32, (64, 256), 1)
    pick = [jnp.where(n == m * 4 + lax.rem(q, 2) * 2 + u, 1.0, 0.0).astype(BF16) for u in range(2)]
    arrive(pan.at[1 - c], e_recv.at[5])
    arrive(g_rows_all.at[c, pl.ds(0, 15)], e_recv.at[2])
    own_tiles = g_rows_all[c].reshape(256, 128)
    score = dot(dot(pick[0], own_tiles).astype(BF16), pan[0])
    score += dot(dot(pick[1], own_tiles).astype(BF16), pan[1])
    for to in range(16):
        s_part[to] = score[to * 4:to * 4 + 4]
    exchange(16, copy_scores)
    copy_pair().start()
    arrive(g_cols_all.at[c, pl.ds(0, 15)], e_recv.at[6])
    copy_pair_cols().start()
    x_far(1)
    x_far(2)
    a_pass((1, 2), (2, 1), 1)
    x_rest(3)
    a_pass((2, 2), (1, 3), 1)
    arrive(g_rows_all.at[1 - c], e_recv.at[3])
    arrive(g_cols_all.at[1 - c], e_recv.at[7])
    m = lax.broadcasted_iota(jnp.int32, (128, 512), 0)
    n = lax.broadcasted_iota(jnp.int32, (128, 512), 1)

    def select(r):
        return jnp.where(n == m * 4 + r, 1.0, 0.0).astype(BF16)

    row_tiles = g_rows_all[...].reshape(512, 128)
    col_tiles = g_cols_all[...].reshape(512, 128)
    g_rows = dot(select(lax.rem(i, 4)), row_tiles).astype(BF16)
    g_cols = jnp.concatenate([dot(select(r), col_tiles).astype(BF16) for r in range(4)], axis=1)
    fish_o[...] = dot(g_rows, g_cols, 0, 0) * (1.0 / 128)

    x_far(3)
    a_pass((2, 3), (3, 1), 1)

    a_pass((3, 2), (3, 3), 2)

    for copy in sent:
        copy.wait_send()
    done_sending(8, copy_in)
    done_sending(8, copy_part)
    done_sending(16, copy_grads)
    done_sending(16, copy_cols)
    copy_pair_cols().wait_send()
    copy_pair().wait_send()
    copy_panels().wait_send()

    arrive(s_recv.at[pl.ds(0, 15)], e_recv.at[4])
    total = s_part[q]
    for step in range(1, 16):
        total = total + s_recv[lax.rem(q + step, 16)]
    score_o[...] = total

    done_sending(16, copy_scores)


def write_out(act, fish, score, act_o, fish_o, score_o, sem):
    copies = [
        pltpu.make_async_copy(src, dst, sem.at[n])
        for n, (src, dst) in enumerate(((act, act_o), (fish, fish_o), (score, score_o)))
    ]
    for copy in copies:
        copy.start()
    for copy in copies:
        copy.wait()


def per_device(acts, cotangent, out_weight, proj_in, proj_out, panels):
    rows, wide = cotangent.shape
    feats = acts.shape[1]
    any_spec = pl.BlockSpec(memory_space=pl.ANY)
    vmem_spec = pl.BlockSpec(memory_space=pltpu.VMEM)
    dma = pltpu.SemaphoreType.DMA
    operands = (acts, cotangent, out_weight, proj_in.T, proj_out.T, panels)
    operands = [pltpu.with_memory_space_constraint(a, pltpu.HBM) for a in operands]
    results = (
        ((rows, feats), BF16),
        ((128, 512), F32),
        ((4, 512), F32),
    )
    held = pl.pallas_call(
        kernel,
        out_shape=tuple(pltpu.VMEM(*r) for r in results),
        in_specs=[any_spec] * 6,
        out_specs=(vmem_spec, vmem_spec, vmem_spec),
        scratch_shapes=[
            pltpu.VMEM((rows, feats), BF16),
            pltpu.VMEM((rows, wide), BF16),
            pltpu.VMEM((feats, 128), BF16),
            pltpu.VMEM((64, feats), BF16),
            pltpu.VMEM((64, wide), BF16),
            pltpu.VMEM((2, 128, 512), BF16),
            pltpu.VMEM((wide, feats), BF16),
            pltpu.VMEM((rows, feats), F32),
            pltpu.VMEM((8, 128, 128), BF16),
            pltpu.VMEM((8, 128, 128), BF16),
            pltpu.VMEM((32, 128), F32),
            pltpu.VMEM((8, 32, 128), F32),
            pltpu.VMEM((8, 16, 128), F32),
            pltpu.VMEM((8, 16, 128), BF16),
            pltpu.VMEM((2, 16, 16, 128), BF16),
            pltpu.VMEM((2, 16, 16, 128), BF16),
            pltpu.VMEM((16, 4, 512), F32),
            pltpu.VMEM((16, 4, 512), F32),
            dma((5,)),
            dma((8,)),
            dma((46,)),
            dma((3, 2)),
            dma((4, 3, 2)),
            dma((4, 4)),
            dma((8, 16)),
            dma((8,)),
            pltpu.SemaphoreType.REGULAR((3,)),
        ],
        compiler_params=pltpu.CompilerParams(
            collective_id=0, has_side_effects=True, vmem_limit_bytes=40 * 1024 * 1024
        ),
        cost_estimate=pl.CostEstimate(
            flops=2 * rows * wide * (feats + 64), bytes_accessed=26 * 2**20, transcendentals=0
        ),
    )(*operands)
    return pl.pallas_call(
        write_out,
        out_shape=tuple(jax.ShapeDtypeStruct(*r) for r in results),
        in_specs=[vmem_spec] * 3,
        out_specs=(any_spec,) * 3,
        scratch_shapes=[dma((3,))],
    )(*(pltpu.with_memory_space_constraint(h, pltpu.VMEM) for h in held))


def solution(mesh):
    return jax.shard_map(
        per_device,
        mesh=mesh,
        in_specs=(
            P("dp", "fisher"),
            P("dp", None),
            P("fisher", "dp"),
            P("fisher", None),
            P(),
            P("dp", "fisher"),
        ),
        out_specs=(P("dp", "fisher"), P("dp", "fisher"), P("dp", "fisher")),
        check_vma=False,
    )
```
